128 devices in a mesh: dp: 128 (over x, y, z, core).
Axes of the slice: x: 4, y: 4, z: 4, core: 2. Of those that a mesh axis runs over, the one named last changes fastest.
Arguments:
- tokens: bfloat16 [24576, 640], P('dp'), may hold values from -6 to 6
- segment_ids: int32 [256, 96], P('dp'), may hold values from 0 to 3, never falling along the last dimension, each value on 1 to 72 neighbouring positions
- cotangent: bfloat16 [24576, 640], P('dp'), may hold values from -6 to 6
- query_weight: bfloat16 [640, 1024], P('dp'), may hold values from -0.25 to 0.25
- key_weight: bfloat16 [640, 256], P('dp'), may hold values from -0.25 to 0.25
- value_weight: bfloat16 [640, 256], P('dp'), may hold values from -0.25 to 0.25
- out_weight: bfloat16 [1024, 640], P(None, 'dp'), may hold values from -0.1875 to 0.1875
- gate_weight: bfloat16 [640, 2048], P('dp'), may hold values from -0.25 to 0.25
- up_weight: bfloat16 [640, 2048], P('dp'), may hold values from -0.25 to 0.25
- down_weight: bfloat16 [2048, 640], P(None, 'dp'), may hold values from -0.125 to 0.125
- input_gain: bfloat16 [640], P('dp'), may hold values from 0.5 to 1.5
- query_gain: bfloat16 [256], P('dp'), may hold values from 0.5 to 1.5
- key_gain: bfloat16 [256], P('dp'), may hold values from 0.5 to 1.5
- post_attn_gain: bfloat16 [640], P('dp'), may hold values from 0.5 to 1.5
- pre_ffn_gain: bfloat16 [640], P('dp'), may hold values from 0.5 to 1.5
- post_ffn_gain: bfloat16 [640], P('dp'), may hold values from 0.5 to 1.5
Outputs:
- layer_out: bfloat16 [24576, 640], P('dp')
- grad_tokens: float32 [24576, 640], P('dp')
- grad_query_weight: float32 [640, 1024], P('dp')
- grad_key_weight: float32 [640, 256], P('dp')
- grad_value_weight: float32 [640, 256], P('dp')
- grad_out_weight: float32 [1024, 640], P(None, 'dp')
- grad_gate_weight: float32 [640, 2048], P('dp')
- grad_up_weight: float32 [640, 2048], P('dp')
- grad_down_weight: float32 [2048, 640], P(None, 'dp')
- grad_input_gain: float32 [640], P('dp')
- grad_query_gain: float32 [256], P('dp')
- grad_key_gain: float32 [256], P('dp')
- grad_post_attn_gain: float32 [640], P('dp')
- grad_pre_ffn_gain: float32 [640], P('dp')
- grad_post_ffn_gain: float32 [640], P('dp')
The draws below stay inside these ranges and needn't reach their ends.
Inputs may be any that keep to these rules, and one draw needn't show every extreme that they name: Along each row of segment_ids the numbers never fall; each sequence is a run of 1 to 72 tokens of one row, and some sequence has exactly 72.
All inputs are finite; a program needn't handle non-finite values.
Results may differ from the reference program's by a relative error of at most 0.025.
Values may be sent and summed in bfloat16 or wider, within the bound.
A program may use at most 128 MiB of HBM per device.

```python
import math
import jax
import jax.numpy as jnp
import numpy as np
from jax import lax

D = 640
HD = 256
QW = 1024
FF = 2048
MB_ROWS = 96
SEGS = 4
SEG_MOST = 72
BLOCKS = 256
TOKENS = 24576


def steps_of(key, shape, cuts, least, largest):
    loudness = 1.0
    for axis_at, shards_of in cuts:
        draws = jax.random.uniform(jax.random.fold_in(jax.random.fold_in(key, 6), axis_at), (shards_of,), jnp.float32, least / len(cuts), largest / len(cuts))
        loudness = loudness * jnp.repeat(jnp.exp(draws), shape[axis_at] // shards_of).reshape((-1,) + (1,) * (len(shape) - 1 - axis_at))
    return loudness


def length_profile(amount, total, bound, lean):
    loads = [(1 << 20) // math.isqrt(rank ** lean) + 1 for rank in range(2, amount + 1)]
    spare, given = total - bound - (amount - 1), [1] * (amount - 1)
    while spare > 0:
        free = [i for i in range(amount - 1) if given[i] < bound]
        pool, remaining = sum([loads[i] for i in free]), spare
        for i in free:
            addition = min(bound - given[i], max(1, remaining * loads[i] // pool), spare)
            given[i] = given[i] + addition
            spare = spare - addition
    return np.array([bound] + given)


def ragged(stream_key, count, total, limit, lean):
    if count == 2:
        one = jax.random.randint(stream_key, (), max(1, total - limit), min(limit, total - 1) + 1)
        return jnp.stack([one, total - one])
    tallies = jnp.asarray(length_profile(count, total, limit, lean), jnp.int32)
    pairs = (count - 1) // 2
    source_of, taker = tallies[1:1 + 2 * pairs:2], tallies[2:2 + 2 * pairs:2]
    slack = jnp.minimum(source_of - 1, limit - taker)
    shifted = jax.random.randint(jax.random.fold_in(stream_key, 1), (pairs,), 0, 1 << 20) % (slack + 1)
    tallies = tallies.at[1:1 + 2 * pairs:2].set(source_of - shifted).at[2:2 + 2 * pairs:2].set(taker + shifted)
    return tallies[jax.random.permutation(jax.random.fold_in(stream_key, 2), count)]


def bell_draw(own_key, extent, scale, bound, split=(), held_as=jnp.bfloat16):
    level = steps_of(own_key, extent, split, -0.22, 0.18) if split else 1.0
    entries = jax.random.normal(own_key, extent, jnp.float32) * scale * level
    return jnp.minimum(jnp.maximum(entries, -bound), bound).astype(held_as)


def setup_inputs(seed: int = 0) -> dict:
    splits = jax.random.split(jax.random.key(seed), 17)
    return {
        "tokens": bell_draw(splits[0], (TOKENS, D), 1.0, 6.0, ((0, 128),)),
        "segment_ids": jax.vmap(lambda own: jnp.searchsorted(jnp.cumsum(ragged(own, SEGS, MB_ROWS, SEG_MOST, 2)), jnp.arange(MB_ROWS), side="right"))(jax.random.split(splits[1], BLOCKS)).reshape((BLOCKS, MB_ROWS)).astype(jnp.int32),
        "cotangent": bell_draw(splits[2], (TOKENS, D), 1.0, 6.0, ((0, 128),)),
        "query_weight": bell_draw(splits[3], (D, QW), D ** -0.5, 0.25, ((0, 128),)),
        "key_weight": bell_draw(splits[4], (D, HD), D ** -0.5, 0.25, ((0, 128),)),
        "value_weight": bell_draw(splits[5], (D, HD), D ** -0.5, 0.25, ((0, 128),)),
        "out_weight": bell_draw(splits[6], (QW, D), QW ** -0.5, 0.1875, ((1, 128),)),
        "gate_weight": bell_draw(splits[7], (D, FF), D ** -0.5, 0.25, ((0, 128),)),
        "up_weight": bell_draw(splits[8], (D, FF), D ** -0.5, 0.25, ((0, 128),)),
        "down_weight": bell_draw(splits[9], (FF, D), FF ** -0.5, 0.125, ((1, 128),)),
        "input_gain": jnp.clip(1.0 + 0.1 * jax.random.normal(splits[10], (D,), jnp.float32), 0.5, 1.5).astype(jnp.bfloat16),
        "query_gain": jnp.clip(1.0 + 0.1 * jax.random.normal(splits[11], (HD,), jnp.float32), 0.5, 1.5).astype(jnp.bfloat16),
        "key_gain": jnp.clip(1.0 + 0.1 * jax.random.normal(splits[12], (HD,), jnp.float32), 0.5, 1.5).astype(jnp.bfloat16),
        "post_attn_gain": jnp.clip(1.0 + 0.1 * jax.random.normal(splits[13], (D,), jnp.float32), 0.5, 1.5).astype(jnp.bfloat16),
        "pre_ffn_gain": jnp.clip(1.0 + 0.1 * jax.random.normal(splits[14], (D,), jnp.float32), 0.5, 1.5).astype(jnp.bfloat16),
        "post_ffn_gain": jnp.clip(1.0 + 0.1 * jax.random.normal(splits[15], (D,), jnp.float32), 0.5, 1.5).astype(jnp.bfloat16),
    }


norm_eps = 1e-06
rope_base = 1000000.0
masked_score = -1e+30
highest = lax.Precision.HIGHEST

@jax.custom_vjp
def low(v):
    return lax.optimization_barrier(v.astype(jnp.bfloat16)).astype(jnp.float32)

@jax.custom_vjp
def low_back(v):
    return v

def low_keep(v):
    return (low(v), None)

def low_pass(kept, grad):
    return (grad,)

def back_keep(v):
    return (v, None)

def back_low(kept, grad):
    return (low(grad),)
low.defvjp(low_keep, low_pass)
low_back.defvjp(back_keep, back_low)

def rms_scale(signal, scale_gain):
    return signal * lax.rsqrt(lax.optimization_barrier(jnp.mean(signal * signal, axis=-1, keepdims=True)) + norm_eps) * scale_gain

def seg_layout(segments):
    seq_length = segments.shape[0]
    token_order = jnp.arange(seq_length, dtype=jnp.int32)
    same_seg = segments[:, None] == segments[None, :]
    earlier = token_order[None, :] < token_order[:, None]
    places = lax.optimization_barrier(jnp.sum((same_seg & earlier).astype(jnp.int32), axis=1))
    allowed = same_seg & (token_order[None, :] <= token_order[:, None])
    return (places, allowed)

def rotate(signal, places):
    feat_width = signal.shape[-1]
    half_width = feat_width // 2
    frequency = jnp.exp(-math.log(rope_base) * 2.0 * jnp.arange(half_width, dtype=jnp.float32) / feat_width)
    angles = places.astype(jnp.float32)[:, None] * frequency[None, :]
    if signal.ndim == 3:
        angles = angles[:, None, :]
    cosine = jnp.cos(angles)
    sine_part = jnp.sin(angles)
    first_half = signal[..., :half_width]
    second_half = signal[..., half_width:]
    return jnp.concatenate([first_half * cosine - second_half * sine_part, second_half * cosine + first_half * sine_part], axis=-1)

def prep_query(query_raw, scale_gain, places):
    return rotate(rms_scale(query_raw, scale_gain), places) * query_raw.shape[-1] ** (-0.5)

def prep_key(key_raw, scale_gain, places):
    return rotate(rms_scale(key_raw, scale_gain), places)

def gated_gelu(gate_proj, up_proj):
    return jax.nn.gelu(gate_proj, approximate=True) * up_proj

def matmul(left, right):
    return jnp.dot(left, right, precision=highest)

def block_forward(params, inputs, segments):
    query_weight, key_weight, value_weight, out_weight, gate_weight, up_weight, down_weight, input_gain, query_gain, key_gain, post_attn_gain, pre_ffn_gain, post_ffn_gain = params
    row_count = inputs.shape[0]
    head_dim = key_weight.shape[1]
    head_count = query_weight.shape[1] // head_dim
    places, allowed = seg_layout(segments)
    h_first = low(rms_scale(inputs, input_gain))
    query_raw = low_back(matmul(h_first, query_weight)).reshape(row_count, head_count, head_dim)
    key_raw = low_back(matmul(h_first, key_weight))
    values = low(low_back(matmul(h_first, value_weight)))
    queries = low(prep_query(query_raw, query_gain, places))
    keys_rot = low(prep_key(key_raw, key_gain, places))
    scores = low_back(jnp.einsum('rhd,cd->hrc', queries, keys_rot, precision=highest))
    scores = jnp.where(allowed[None], scores, masked_score)
    row_max = lax.optimization_barrier(jnp.max(scores, axis=-1, keepdims=True))
    exp_scores = jnp.exp(scores - row_max)
    attn_probs = low(exp_scores / lax.optimization_barrier(jnp.sum(exp_scores, axis=-1, keepdims=True)))
    context = low(low_back(jnp.einsum('hrc,cd->rhd', attn_probs, values, precision=highest)))
    context = context.reshape(row_count, head_count * head_dim)
    attn_out = low_back(matmul(context, out_weight))
    mid_stream = inputs + rms_scale(attn_out, post_attn_gain)
    h_second = low(rms_scale(mid_stream, pre_ffn_gain))
    gate_proj = low_back(matmul(h_second, gate_weight))
    up_proj = low_back(matmul(h_second, up_weight))
    hidden = low(gated_gelu(gate_proj, up_proj))
    mixed_out = low_back(matmul(hidden, down_weight))
    return mid_stream + rms_scale(mixed_out, post_ffn_gain)

def reference(tokens, segment_ids, cotangent, query_weight, key_weight, value_weight, out_weight, gate_weight, up_weight, down_weight, input_gain, query_gain, key_gain, post_attn_gain, pre_ffn_gain, post_ffn_gain):
    params = tuple((item.astype(jnp.float32) for item in (query_weight, key_weight, value_weight, out_weight, gate_weight, up_weight, down_weight, input_gain, query_gain, key_gain, post_attn_gain, pre_ffn_gain, post_ffn_gain)))
    target = max(1, 4096 // MB_ROWS)
    pow_two = 1 << target.bit_length() - 1
    group_size = math.gcd(BLOCKS, pow_two)
    step_count = BLOCKS // group_size
    inputs = tokens.astype(jnp.float32).reshape(step_count, group_size, MB_ROWS, D)
    segments = segment_ids.reshape(step_count, group_size, MB_ROWS)
    upstream = cotangent.astype(jnp.float32).reshape(step_count, group_size, MB_ROWS, D)
    group_forward = jax.checkpoint(jax.vmap(block_forward, in_axes=(None, 0, 0)))

    def whole_layer(param_set, inputs_all):
        return lax.map(lambda block_pair: group_forward(param_set, block_pair[0], block_pair[1]), (inputs_all, segments))
    outputs, pullback = jax.vjp(whole_layer, params, inputs)
    grad_params, grad_inputs = pullback(upstream)
    return (outputs.reshape(TOKENS, D).astype(jnp.bfloat16), grad_inputs.reshape(TOKENS, D), grad_params[0], grad_params[1], grad_params[2], grad_params[3], grad_params[4], grad_params[5], grad_params[6], grad_params[7], grad_params[8], grad_params[9], grad_params[10], grad_params[11], grad_params[12])
```

```python
import functools
import math

import jax
import jax.numpy as jnp
from jax import lax
from jax.experimental import pallas as pl
from jax.experimental.pallas import tpu as pltpu
from jax.sharding import PartitionSpec as P

BF = jnp.bfloat16
F32 = jnp.float32
MESH = pl.DeviceIdType.MESH


class Place:
    def __init__(self):
        me = lax.axis_index("dp")
        self.me = me
        self.c = lax.rem(me, 2)
        self.z = lax.rem(lax.div(me, 2), 4)
        self.y = lax.rem(lax.div(me, 8), 4)
        self.x = lax.div(me, 32)
        self.yl = lax.rem(self.y, 2)
        self.yh = lax.div(self.y, 2)
        self.at = {"x": self.x, "y": self.y, "z": self.z}

    def device(self, x, y, z, c):
        return ((x * 4 + y) * 4 + z) * 2 + c

    def moved(self, axis, by):
        return lax.rem(self.at[axis] + by, 4)

    def peer(self, axis, by):
        spot = dict(self.at)
        spot[axis] = self.moved(axis, by)
        return self.device(spot["x"], spot["y"], spot["z"], self.c)

    def sibling(self):
        return self.device(self.x, self.y, self.z, 1 - self.c)

    def group_peers(self):
        found = []
        for dyl in range(2):
            for dz in range(4):
                for dc in range(2):
                    if dyl or dz or dc:
                        yl = lax.rem(self.yl + dyl, 2)
                        z = lax.rem(self.z + dz, 4)
                        c = lax.rem(self.c + dc, 2)
                        found.append(
                            (
                                self.device(self.x, self.yh * 2 + yl, z, c),
                                c * 8 + yl * 4 + z,
                                yl * 8 + z * 2 + c,
                            )
                        )
        return found

    def slot(self):
        return self.c * 8 + self.yl * 4 + self.z

    def natural(self):
        return self.yl * 8 + self.z * 2 + self.c

    def greet(self):
        others = [item[0] for item in self.group_peers()]
        others += [self.peer("x", by) for by in (1, 2, 3)]
        others += [
            self.device(self.x, (1 - self.yh) * 2 + yl, self.z, self.c) for yl in range(2)
        ]
        barrier = pltpu.get_barrier_semaphore()
        for other in others:
            pl.semaphore_signal(barrier, inc=1, device_id=(other,), device_id_type=MESH)
        pl.semaphore_wait(barrier, len(others))


def region(select, half=None):
    index = []
    for axis in "xyz":
        value = select[axis]
        if value is None:
            cut = half is not None
            if axis == "y":
                index += [pl.ds(half, 1) if cut else slice(None), slice(None)]
            else:
                index.append(pl.ds(2 * half, 2) if cut else slice(None))
            half = None
        elif axis == "y":
            index += [lax.div(value, 2), lax.rem(value, 2)]
        else:
            index.append(value)
    return tuple(index)


def half_shape(whole):
    shape, cut = [], True
    for axis in "xyz":
        if axis in whole:
            if axis == "y":
                shape += [1 if cut else 2, 2]
            else:
                shape.append(2 if cut else 4)
            cut = False
    return tuple(shape)


class Sender:
    def __init__(self, send_sems, recv_sems):
        self.send_sems, self.recv_sems = send_sems, recv_sems
        self.used = 0
        self.open = []

    def send(self, source, target, device):
        copy = pltpu.make_async_remote_copy(
            src_ref=source,
            dst_ref=target,
            send_sem=self.send_sems.at[self.used],
            recv_sem=self.recv_sems.at[self.used],
            device_id=(device,),
            device_id_type=MESH,
        )
        self.used += 1
        copy.start()
        self.open.append(copy)
        return copy

    def finish(self):
        for copy in self.open:
            copy.wait_send()
        self.open = []


def gather_class(place, sender, ref, rows, order):
    tail = (pl.ds(rows[0], rows[1]), slice(None))

    def view(select, half=None):
        return ref.at[(place.c,) + region(select, half) + tail]

    def select_for(step, value):
        chosen = {}
        for at, axis in enumerate(order):
            chosen[axis] = None if at < step else value if at == step else place.at[axis]
        return chosen

    def push(part, device):
        return sender.send(part, part, device)

    axis = order[0]
    own = view(select_for(0, place.at[axis]))
    first = [push(own, place.peer(axis, by)) for by in (1, 3, 2)]
    yield
    for copy in first:
        copy.wait_recv()
    twin = []
    for step in (1, 2):
        axis = order[step]
        last = step == 2
        right, left = place.peer(axis, 1), place.peer(axis, 3)
        mine = select_for(step, place.at[axis])
        of_right = select_for(step, place.moved(axis, 1))
        of_left = select_for(step, place.moved(axis, 3))
        of_far = select_for(step, place.moved(axis, 2))
        r0 = push(view(mine, 0), right)
        l1 = push(view(mine, 1), left)
        r1 = push(view(mine, 1), right)
        l0 = push(view(mine, 0), left)
        if last:
            twin.append(push(view(mine), place.sibling()))
        yield
        r0.wait_recv()
        f0 = push(view(of_left, 0), right)
        l1.wait_recv()
        f1 = push(view(of_right, 1), left)
        yield
        r1.wait_recv()
        if last:
            twin.append(push(view(of_left), place.sibling()))
        l0.wait_recv()
        if last:
            twin.append(push(view(of_right), place.sibling()))
        yield
        f0.wait_recv()
        if last:
            twin.append(push(view(of_far, 0), place.sibling()))
        f1.wait_recv()
        if last:
            twin.append(push(view(of_far, 1), place.sibling()))
    yield
    for copy in twin:
        copy.wait_recv()


GATHER_COPIES = 20
SCATTER_COPIES = 19


def scatter_class(place, sender, ref, twin_ref, landing, rows, order):
    tail = (pl.ds(rows[0], rows[1]), slice(None))
    order = order[::-1]

    def at(select, half=None):
        return (place.c,) + region(select, half) + tail

    def select_for(step, value):
        chosen = {}
        for where, axis in enumerate(order):
            chosen[axis] = (
                place.at[axis] if where < step else value if where == step else None
            )
        return chosen

    def add(index, *others):
        total = ref[index].astype(F32)
        for other in others:
            total = total + other.astype(F32)
        ref[index] = total.astype(BF)

    axis = order[0]
    pieces = []
    for by in (2, 1, 3, 0):
        part = region(select_for(0, place.moved(axis, by))) + tail
        pieces.append(
            (part, sender.send(ref.at[(1 - place.c,) + part], twin_ref.at[part], place.sibling()))
        )
    yield

    def joined(which):
        if pieces is None:
            return
        part, copy = pieces[which]
        copy.wait_recv()
        add((place.c,) + part, twin_ref[part])

    for step in (0, 1):
        axis = order[step]
        land = landing[step]
        right, left = place.peer(axis, 1), place.peer(axis, 3)
        mine = select_for(step, place.at[axis])
        to_right = select_for(step, place.moved(axis, 1))
        to_left = select_for(step, place.moved(axis, 3))
        far = select_for(step, place.moved(axis, 2))
        joined(0)
        f0 = sender.send(ref.at[at(far, 0)], land.at[0], right)
        f1 = sender.send(ref.at[at(far, 1)], land.at[1], left)
        joined(1)
        r1 = sender.send(ref.at[at(to_right, 1)], land.at[2], right)
        joined(2)
        l0 = sender.send(ref.at[at(to_left, 0)], land.at[3], left)
        yield
        f0.wait_recv()
        add(at(to_right, 0), land[0])
        r0 = sender.send(ref.at[at(to_right, 0)], land.at[4], right)
        f1.wait_recv()
        add(at(to_left, 1), land[1])
        l1 = sender.send(ref.at[at(to_left, 1)], land.at[5], left)
        joined(3)
        pieces = None
        yield
        r1.wait_recv()
        l0.wait_recv()
        r0.wait_recv()
        l1.wait_recv()
        add(at(mine, 0), land[4], land[3])
        add(at(mine, 1), land[2], land[5])
    axis = order[2]
    land = landing[2]
    sent = [
        sender.send(
            ref.at[at(select_for(2, place.moved(axis, by)))], land.at[by - 1], place.peer(axis, by)
        )
        for by in (1, 3, 2)
    ]
    yield
    for copy in sent:
        copy.wait_recv()
    add(at(select_for(2, place.at[axis])), land[0], land[1], land[2])


def landing_shapes(rows, order):
    back = order[::-1]
    return [
        pltpu.VMEM((6,) + half_shape(back[1:]) + (rows, 128), BF),
        pltpu.VMEM((6,) + half_shape(back[2:]) + (rows, 128), BF),
        pltpu.VMEM((3, rows, 128), BF),
    ]


def take_turns(tasks):
    tasks = list(tasks)
    while tasks:
        still = []
        for task in tasks:
            try:
                next(task)
                still.append(task)
            except StopIteration:
                pass
        tasks = still


def picker(part, transposed=False):
    i = lax.broadcasted_iota(jnp.int32, (80, 512), 0)
    j = lax.broadcasted_iota(jnp.int32, (80, 512), 1)
    n = lax.shift_right_logical(j, 5)
    r = lax.bitwise_and(j, 7)
    m = lax.bitwise_and(lax.shift_right_logical(j, 3), 3)
    hit = (m == part) & (r < 5) & (i == n * 5 + r)
    return jnp.where(hit, 1.0, 0.0).astype(BF)


def stacked(parts):
    pad = jnp.zeros((3, 128), F32)
    return jnp.concatenate(
        [item for part in parts for item in (part.astype(F32), pad)], axis=0
    )


CLASSES = (
    (0, 0, 32, "xyz"),
    (0, 32, 48, "yzx"),
    (4, 0, 32, "zxy"),
    (1, 0, 80, "xyz"),
    (2, 0, 80, "yzx"),
    (3, 0, 80, "zxy"),
)
BLOCK_ROWS = (80, 80, 80, 80, 32)


def fill_messages(q, o, k, v, g, u, d, gains, msgs, kv_block):
    for slot in range(16):
        lanes = slice(slot * 128, slot * 128 + 128)
        narrow = slice(slot % 8 * 128, slot % 8 * 128 + 128)
        qo = q[:, narrow] if slot < 8 else o[:, narrow]
        msgs[slot] = stacked([g[:, lanes], u[:, lanes], d[:, lanes], qo]).astype(BF)
    flat = stacked([k[:, 0:128], k[:, 128:256], v[:, 0:128], v[:, 128:256]])
    row = lax.broadcasted_iota(jnp.int32, (32, 128), 0)
    for at, target in enumerate(GAIN_ROWS):
        flat = jnp.where(row == target, gains[at : at + 1, :], flat)
    kv_block[...] = flat.astype(BF)


GAIN_ROWS = (5, 13, 21, 29, 6, 14)


def exchange_in(place, sender, msgs, recv, bufs, kv_block):
    copies = [
        sender.send(msgs.at[slot], recv.at[place.natural()], device)
        for device, slot, _ in place.group_peers()
    ]
    recv[place.natural()] = msgs[place.slot()]
    spot = (place.c, place.x, place.yh, place.yl, place.z)
    bufs[4][spot] = kv_block[...]
    for copy in copies:
        copy.wait_recv()
    flat = recv[...].reshape(512, 128)
    for part, buf in ((3, bufs[0]), (0, bufs[1]), (1, bufs[2]), (2, bufs[3])):
        buf[spot] = jnp.dot(picker(part), flat, preferred_element_type=F32).astype(BF)


def spread_rows(buf, row):
    takes = []
    for x in range(4):
        for yh in range(2):
            for yl in range(2):
                both = [
                    jnp.concatenate(
                        [buf[c, x, yh, yl, z, row // 8 * 8 : row // 8 * 8 + 8, :] for c in range(2)], 0
                    )
                    for z in range(4)
                ]
                takes += both
    every = jnp.concatenate(takes, axis=0)
    i = lax.broadcasted_iota(jnp.int32, (128, 1024), 0)
    j = lax.broadcasted_iota(jnp.int32, (128, 1024), 1)
    pick = jnp.where(j == i * 8 + row % 8, 1.0, 0.0).astype(BF)
    return jnp.dot(pick, every, preferred_element_type=F32)


def gain_line(buf, row, each, width):
    held = spread_rows(buf, row)
    count = lax.broadcasted_iota(jnp.int32, (128, width), 0)
    lane = lax.broadcasted_iota(jnp.int32, (128, width), 1)
    place_in = lane - count * each
    r = lax.broadcasted_iota(jnp.int32, (128, width), 0)
    rep = jnp.where(lax.rem(lane, each) == r, 1.0, 0.0).astype(BF)
    lined = jnp.dot(held.astype(BF), rep, preferred_element_type=F32)
    lined = jnp.where((place_in >= 0) & (place_in < each), lined, 0.0)
    return jnp.sum(lined, axis=0, keepdims=True)


def kv_group(buf, g, part):
    x, yh = lax.div(g, 2), lax.rem(g, 2)
    blocks = [
        buf[c, x, yh, yl, z] for yl in range(2) for z in range(4) for c in range(2)
    ]
    return jnp.dot(picker(part), jnp.concatenate(blocks, axis=0), preferred_element_type=F32)


def gather_kernel(
    q, k, v, o, g, u, d, gains, qo_out, g_out, u_out, d_out, kv_out, gain_out,
    qo_buf, g_buf, u_buf, d_buf, kv_buf, msgs, recv, kv_block, send_sems, recv_sems, out_sems,
):
    place = Place()
    fill_messages(q, o, k, v, g, u, d, gains, msgs, kv_block)
    place.greet()
    sender = Sender(send_sems, recv_sems)
    bufs = (qo_buf, g_buf, u_buf, d_buf, kv_buf)
    exchange_in(place, sender, msgs, recv, bufs, kv_block)
    take_turns(
        gather_class(place, sender, bufs[which], (first, count), order)
        for which, first, count, order in CLASSES
    )
    outs = []
    for at, (buf, out) in enumerate(((qo_buf, qo_out), (g_buf, g_out), (u_buf, u_out), (d_buf, d_out))):
        for slot in range(16):
            c, yl, z = slot // 8, slot // 4 % 2, slot % 4
            copy = pltpu.make_async_copy(
                buf.at[c, :, :, yl, z],
                out.at[:, :, :, pl.ds(slot * 128, 128)],
                out_sems.at[at * 16 + slot],
            )
            copy.start()
            outs.append(copy)
    for part in range(4):
        for group in range(8):
            kv_out[group * 80 : group * 80 + 80, part * 128 : part * 128 + 128] = kv_group(
                kv_buf, group, part
            ).astype(BF)
    gain_out[...] = jnp.zeros((8, 640), F32)
    for at, row in enumerate(GAIN_ROWS):
        if at < 4:
            gain_out[at : at + 1, :] = gain_line(kv_buf, row, 5, 640)
        else:
            gain_out[at : at + 1, 0:256] = gain_line(kv_buf, row, 2, 256)
    for copy in outs:
        copy.wait()
    sender.finish()


def gather_weights(q, k, v, o_t, g, u, d_t, gains):
    grid = (2, 4, 2, 2, 4)
    vm = pl.BlockSpec(memory_space=pltpu.VMEM)
    hbm = pl.BlockSpec(memory_space=pl.ANY)
    copies = 15 + GATHER_COPIES * len(CLASSES)
    wide = jax.ShapeDtypeStruct((4, 2, 80, 2048), BF)
    return pl.pallas_call(
        gather_kernel,
        out_shape=(wide, wide, wide, wide,
                   jax.ShapeDtypeStruct((640, 512), BF), jax.ShapeDtypeStruct((8, 640), F32)),
        in_specs=[vm] * 8,
        out_specs=(hbm, hbm, hbm, hbm, vm, vm),
        scratch_shapes=[pltpu.VMEM(grid + (rows, 128), BF) for rows in BLOCK_ROWS]
        + [
            pltpu.VMEM((16, 32, 128), BF),
            pltpu.VMEM((16, 32, 128), BF),
            pltpu.VMEM((32, 128), BF),
            pltpu.SemaphoreType.DMA((copies,)),
            pltpu.SemaphoreType.DMA((copies,)),
            pltpu.SemaphoreType.DMA((64,)),
        ],
        compiler_params=pltpu.CompilerParams(
            collective_id=0, has_side_effects=True, vmem_limit_bytes=56 << 20
        ),
    )(q, k, v, o_t, g, u, d_t, gains)


def spread_gain(line, each):
    width = line.shape[1]
    count = lax.broadcasted_iota(jnp.int32, (128, width), 0)
    lane = lax.broadcasted_iota(jnp.int32, (128, width), 1)
    inside = lane - count * each
    kept = jnp.where((inside >= 0) & (inside < each), jnp.broadcast_to(line, (128, width)), 0.0)
    r = lax.broadcasted_iota(jnp.int32, (width, 128), 0)
    to = lax.broadcasted_iota(jnp.int32, (width, 128), 1)
    pick = jnp.where(lax.rem(r, each) == to, 1.0, 0.0).astype(BF)
    return jnp.dot(kept.astype(BF), pick, preferred_element_type=F32)


def fill_kv_gradient(kv, gain_lines, buf):
    gains = [spread_gain(line, 5 if at < 4 else 2) for at, line in enumerate(gain_lines)]
    row = lax.broadcasted_iota(jnp.int32, (512, 128), 0)
    seat = lax.bitwise_and(row, 31)
    n = lax.broadcasted_iota(jnp.int32, (512, 16), 0)
    m = lax.broadcasted_iota(jnp.int32, (512, 16), 1)
    repeat = jnp.where(lax.shift_right_logical(n, 5) == m, 1.0, 0.0).astype(BF)
    for group in range(8):
        flat = jnp.zeros((512, 128), F32)
        for part in range(4):
            flat = flat + lax.dot_general(
                picker(part), kv(group, part), (((0,), (0,)), ((), ())), preferred_element_type=F32
            )
        for at, target in enumerate(GAIN_ROWS):
            own = gains[at][group * 16 : group * 16 + 16].astype(BF)
            flat = jnp.where(
                seat == target, jnp.dot(repeat, own, preferred_element_type=F32), flat
            )
        flat = flat.astype(BF)
        for n16 in range(16):
            yl, z, c = n16 // 8, n16 // 2 % 4, n16 % 2
            buf[c, group // 2, group % 2, yl, z] = flat[n16 * 32 : n16 * 32 + 32]


def exchange_out(place, sender, msgs, recv, bufs):
    spot = (place.c, place.x, place.yh, place.yl, place.z)
    flat = jnp.zeros((512, 128), F32)
    for part, buf in ((3, bufs[0]), (0, bufs[1]), (1, bufs[2]), (2, bufs[3])):
        flat = flat + lax.dot_general(
            picker(part), buf[spot], (((0,), (0,)), ((), ())), preferred_element_type=F32
        )
    msgs[...] = flat.astype(BF).reshape(16, 32, 128)
    copies = [
        sender.send(msgs.at[natural], recv.at[place.slot()], device)
        for device, _, natural in place.group_peers()
    ]
    recv[place.slot()] = msgs[place.natural()]
    for copy in copies:
        copy.wait_recv()


def write_shards(place, recv, bufs, q_out, k_out, v_out, o_out, g_out, u_out, d_out, gain_out):
    for slot in range(16):
        part = recv[slot].astype(F32)
        lanes = slice(slot * 128, slot * 128 + 128)
        narrow = slice(slot % 8 * 128, slot % 8 * 128 + 128)
        g_out[:, lanes] = part[0:5]
        u_out[:, lanes] = part[8:13]
        d_out[:, lanes] = part[16:21]
        (q_out if slot < 8 else o_out)[:, narrow] = part[24:29]
    spot = (place.c, place.x, place.yh, place.yl, place.z)
    flat = bufs[4][spot].astype(F32)
    k_out[:, 0:128] = flat[0:5]
    k_out[:, 128:256] = flat[8:13]
    v_out[:, 0:128] = flat[16:21]
    v_out[:, 128:256] = flat[24:29]
    gain_out[...] = jnp.concatenate(
        [flat[row : row + 1] for row in GAIN_ROWS] + [jnp.zeros((2, 128), F32)], axis=0
    )


def scatter_kernel(
    qo, g, u, d, kv, gain_lines,
    q_out, k_out, v_out, o_out, g_out, u_out, d_out, gain_out,
    *scratch,
):
    bufs, twins = scratch[0:5], scratch[5:10]
    landings = scratch[10 : 10 + 3 * len(CLASSES)]
    msgs, recv, send_sems, recv_sems, in_sems = scratch[10 + 3 * len(CLASSES) :]
    place = Place()
    ins = []
    for at, (buf, source) in enumerate(((bufs[0], qo), (bufs[1], g), (bufs[2], u), (bufs[3], d))):
        for slot in range(16):
            c, yl, z = slot // 8, slot // 4 % 2, slot % 4
            copy = pltpu.make_async_copy(
                source.at[:, :, :, pl.ds(slot * 128, 128)],
                buf.at[c, :, :, yl, z],
                in_sems.at[at * 16 + slot],
            )
            copy.start()
            ins.append(copy)
    fill_kv_gradient(
        lambda group, part: kv[group * 80 : group * 80 + 80, part * 128 : part * 128 + 128],
        [gain_lines[at : at + 1, 0 : (640 if at < 4 else 256)] for at in range(6)],
        bufs[4],
    )
    for copy in ins:
        copy.wait()
    place.greet()
    sender = Sender(send_sems, recv_sems)
    take_turns(
        scatter_class(
            place, sender, bufs[which], twins[which], landings[3 * at : 3 * at + 3], (first, count), order
        )
        for at, (which, first, count, order) in enumerate(CLASSES)
    )
    exchange_out(place, sender, msgs, recv, bufs)
    write_shards(place, recv, bufs, q_out, k_out, v_out, o_out, g_out, u_out, d_out, gain_out)
    sender.finish()


def scatter_gradients(qo, g, u, d, kv, gain_lines):
    vm = pl.BlockSpec(memory_space=pltpu.VMEM)
    hbm = pl.BlockSpec(memory_space=pl.ANY)
    copies = 15 + SCATTER_COPIES * len(CLASSES)
    shape = lambda *dims: jax.ShapeDtypeStruct(dims, F32)
    scratch = [pltpu.VMEM((2, 4, 2, 2, 4, rows, 128), BF) for rows in BLOCK_ROWS]
    scratch += [pltpu.VMEM((4, 2, 2, 4, rows, 128), BF) for rows in BLOCK_ROWS]
    for _, _, count, order in CLASSES:
        scratch += landing_shapes(count, order)
    return pl.pallas_call(
        scatter_kernel,
        out_shape=(shape(5, 1024), shape(5, 256), shape(5, 256), shape(5, 1024),
                   shape(5, 2048), shape(5, 2048), shape(5, 2048), shape(8, 128)),
        in_specs=[hbm] * 4 + [vm] * 2,
        out_specs=(vm,) * 8,
        scratch_shapes=scratch
        + [
            pltpu.VMEM((16, 32, 128), BF),
            pltpu.VMEM((16, 32, 128), BF),
            pltpu.SemaphoreType.DMA((copies,)),
            pltpu.SemaphoreType.DMA((copies,)),
            pltpu.SemaphoreType.DMA((64,)),
        ],
        compiler_params=pltpu.CompilerParams(
            collective_id=1, has_side_effects=True, vmem_limit_bytes=56 << 20
        ),
    )(qo, g, u, d, kv, gain_lines)


norm_eps = 1e-06
rope_base = 1000000.0
masked_score = -1e30


def rms_scale(signal, scale_gain):
    return (
        signal
        * lax.rsqrt(jnp.mean(signal * signal, axis=-1, keepdims=True) + norm_eps)
        * scale_gain
    )


def seg_layout(segments):
    seq_length = segments.shape[0]
    token_order = jnp.arange(seq_length, dtype=jnp.int32)
    same_seg = segments[:, None] == segments[None, :]
    earlier = token_order[None, :] < token_order[:, None]
    places = jnp.sum((same_seg & earlier).astype(jnp.int32), axis=1)
    allowed = same_seg & (token_order[None, :] <= token_order[:, None])
    return (places, allowed)


def rotate(signal, places):
    feat_width = signal.shape[-1]
    half_width = feat_width // 2
    frequency = jnp.exp(
        -math.log(rope_base) * 2.0 * jnp.arange(half_width, dtype=jnp.float32) / feat_width
    )
    angles = places.astype(jnp.float32)[:, None] * frequency[None, :]
    if signal.ndim == 3:
        angles = angles[:, None, :]
    cosine = jnp.cos(angles)
    sine_part = jnp.sin(angles)
    first_half = signal[..., :half_width]
    second_half = signal[..., half_width:]
    return jnp.concatenate(
        [
            first_half * cosine - second_half * sine_part,
            second_half * cosine + first_half * sine_part,
        ],
        axis=-1,
    )


def prep_query(query_raw, scale_gain, places):
    return rotate(rms_scale(query_raw, scale_gain), places) * query_raw.shape[-1] ** (-0.5)


def prep_key(key_raw, scale_gain, places):
    return rotate(rms_scale(key_raw, scale_gain), places)


def gated_gelu(gate_proj, up_proj):
    return jax.nn.gelu(gate_proj, approximate=True) * up_proj


def product(left, right):
    return jnp.dot(left, right, preferred_element_type=jnp.float32)


def forward_micro(params, inputs, segments):
    (
        query_weight,
        key_weight,
        value_weight,
        out_weight,
        gate_weight,
        up_weight,
        down_weight,
        input_gain,
        query_gain,
        key_gain,
        post_attn_gain,
        pre_ffn_gain,
        post_ffn_gain,
    ) = params
    row_count = inputs.shape[0]
    head_dim = key_weight.shape[1]
    head_count = query_weight.shape[1] // head_dim
    places, allowed = seg_layout(segments)
    h_first = rms_scale(inputs, input_gain.astype(jnp.float32)).astype(jnp.bfloat16)
    query_raw = product(h_first, query_weight).reshape(row_count, head_count, head_dim)
    key_raw = product(h_first, key_weight)
    values = product(h_first, value_weight).astype(jnp.bfloat16)
    queries = prep_query(query_raw, query_gain.astype(jnp.float32), places).astype(jnp.bfloat16)
    keys_rot = prep_key(key_raw, key_gain.astype(jnp.float32), places).astype(jnp.bfloat16)
    scores = jnp.einsum("rhd,cd->hrc", queries, keys_rot, preferred_element_type=jnp.float32)
    scores = jnp.where(allowed[None], scores, masked_score)
    row_max = jnp.max(scores, axis=-1, keepdims=True)
    exp_scores = jnp.exp(scores - row_max)
    row_total = jnp.sum(exp_scores, axis=-1, keepdims=True)
    attn_probs = (exp_scores / row_total).astype(jnp.bfloat16)
    log_total = row_max + jnp.log(row_total)
    context = jnp.einsum("hrc,cd->rhd", attn_probs, values, preferred_element_type=jnp.float32)
    context = context.astype(jnp.bfloat16).reshape(row_count, head_count * head_dim)
    attn_out = product(context, out_weight)
    mid_stream = inputs + rms_scale(attn_out, post_attn_gain.astype(jnp.float32))
    h_second = rms_scale(mid_stream, pre_ffn_gain.astype(jnp.float32)).astype(jnp.bfloat16)
    gate_proj = product(h_second, gate_weight)
    up_proj = product(h_second, up_weight)
    hidden = gated_gelu(gate_proj, up_proj).astype(jnp.bfloat16)
    mixed_out = product(hidden, down_weight)
    result = mid_stream + rms_scale(mixed_out, post_ffn_gain.astype(jnp.float32))
    record = (
        h_first,
        query_raw,
        key_raw,
        values,
        queries,
        keys_rot,
        log_total,
        places,
        allowed,
        context,
        attn_out,
        mid_stream,
        h_second,
        gate_proj,
        up_proj,
        hidden,
        mixed_out,
    )
    return (result, record)


def backward_micro(params, inputs, record, upstream):
    (
        query_weight,
        key_weight,
        value_weight,
        out_weight,
        gate_weight,
        up_weight,
        down_weight,
        input_gain,
        query_gain,
        key_gain,
        post_attn_gain,
        pre_ffn_gain,
        post_ffn_gain,
    ) = params
    (
        h_first,
        query_raw,
        key_raw,
        values,
        queries,
        keys_rot,
        log_total,
        places,
        allowed,
        context,
        attn_out,
        mid_stream,
        h_second,
        gate_proj,
        up_proj,
        hidden,
        mixed_out,
    ) = record
    row_count = inputs.shape[0]
    head_dim = key_weight.shape[1]
    head_count = query_weight.shape[1] // head_dim
    _, pullback = jax.vjp(rms_scale, mixed_out, post_ffn_gain.astype(jnp.float32))
    grad_mixed, grad_post_ffn = pullback(upstream)
    grad_mixed = grad_mixed.astype(jnp.bfloat16)
    grad_hidden = jnp.einsum(
        "rd,fd->rf", grad_mixed, down_weight, preferred_element_type=jnp.float32
    )
    _, pullback = jax.vjp(gated_gelu, gate_proj, up_proj)
    grad_gate, grad_up = pullback(grad_hidden)
    grad_gate = grad_gate.astype(jnp.bfloat16)
    grad_up = grad_up.astype(jnp.bfloat16)
    grad_second = jnp.einsum(
        "rf,df->rd", grad_gate, gate_weight, preferred_element_type=jnp.float32
    ) + jnp.einsum("rf,df->rd", grad_up, up_weight, preferred_element_type=jnp.float32)
    _, pullback = jax.vjp(rms_scale, mid_stream, pre_ffn_gain.astype(jnp.float32))
    grad_mid_part, grad_pre_ffn = pullback(grad_second)
    grad_mid = upstream + grad_mid_part
    _, pullback = jax.vjp(rms_scale, attn_out, post_attn_gain.astype(jnp.float32))
    grad_attn, grad_post_attn = pullback(grad_mid)
    grad_attn = grad_attn.astype(jnp.bfloat16)
    grad_context = jnp.einsum(
        "rd,qd->rq", grad_attn, out_weight, preferred_element_type=jnp.float32
    )
    grad_context = grad_context.astype(jnp.bfloat16).reshape(row_count, head_count, head_dim)
    scores = jnp.einsum("rhd,cd->hrc", queries, keys_rot, preferred_element_type=jnp.float32)
    scores = jnp.where(allowed[None], scores, masked_score)
    attn_probs = jnp.exp(scores - log_total)
    grad_probs = jnp.einsum("rhd,cd->hrc", grad_context, values, preferred_element_type=jnp.float32)
    grad_values = jnp.einsum(
        "hrc,rhd->cd",
        attn_probs.astype(jnp.bfloat16),
        grad_context,
        preferred_element_type=jnp.float32,
    ).astype(jnp.bfloat16)
    grad_scores = attn_probs * (
        grad_probs - jnp.sum(attn_probs * grad_probs, axis=-1, keepdims=True)
    )
    grad_scores = grad_scores.astype(jnp.bfloat16)
    grad_queries = jnp.einsum(
        "hrc,cd->rhd", grad_scores, keys_rot, preferred_element_type=jnp.float32
    )
    grad_keys = jnp.einsum("hrc,rhd->cd", grad_scores, queries, preferred_element_type=jnp.float32)
    _, pullback = jax.vjp(
        lambda raw_part, gain_part: prep_query(raw_part, gain_part, places),
        query_raw,
        query_gain.astype(jnp.float32),
    )
    grad_qraw, grad_qgain = pullback(grad_queries)
    _, pullback = jax.vjp(
        lambda raw_part, gain_part: prep_key(raw_part, gain_part, places),
        key_raw,
        key_gain.astype(jnp.float32),
    )
    grad_kraw, grad_kgain = pullback(grad_keys)
    grad_qraw = grad_qraw.reshape(row_count, head_count * head_dim).astype(jnp.bfloat16)
    grad_kraw = grad_kraw.astype(jnp.bfloat16)
    grad_first = (
        jnp.einsum("rq,dq->rd", grad_qraw, query_weight, preferred_element_type=jnp.float32)
        + jnp.einsum("rq,dq->rd", grad_kraw, key_weight, preferred_element_type=jnp.float32)
        + jnp.einsum("rq,dq->rd", grad_values, value_weight, preferred_element_type=jnp.float32)
    )
    _, pullback = jax.vjp(rms_scale, inputs, input_gain.astype(jnp.float32))
    grad_in_part, grad_input = pullback(grad_first)
    grad_inputs = grad_mid + grad_in_part
    saved = (
        h_first,
        grad_qraw,
        grad_kraw,
        grad_values,
        context,
        grad_attn,
        h_second,
        grad_gate,
        grad_up,
        hidden,
        grad_mixed,
    )
    width_gains = (grad_input, grad_post_attn, grad_pre_ffn, grad_post_ffn)
    head_gains = (grad_qgain, grad_kgain)
    return (grad_inputs, saved, width_gains, head_gains)


def per_device(
    tokens,
    segment_ids,
    cotangent,
    query_weight,
    key_weight,
    value_weight,
    out_weight,
    gate_weight,
    up_weight,
    down_weight,
    input_gain,
    query_gain,
    key_gain,
    post_attn_gain,
    pre_ffn_gain,
    post_ffn_gain,
):
    micro_count, row_count = segment_ids.shape
    feat_width = tokens.shape[1]
    inputs = tokens.astype(F32).reshape(micro_count, row_count, feat_width)
    upstream = cotangent.astype(F32).reshape(micro_count, row_count, feat_width)
    gains = (input_gain, post_attn_gain, pre_ffn_gain, post_ffn_gain, query_gain, key_gain)
    gain_rows = jnp.stack([jnp.pad(item.astype(F32), (0, 128 - item.shape[0])) for item in gains])
    gain_rows = jnp.pad(gain_rows, ((0, 2), (0, 0)))
    qo, gw, uw, dw, kv, lines = gather_weights(
        query_weight, key_weight, value_weight, out_weight.T, gate_weight, up_weight, down_weight.T, gain_rows
    )
    qo, gw, uw, dw = (item.reshape(640, 2048) for item in (qo, gw, uw, dw))
    params = (
        qo[:, :1024], kv[:, :256], kv[:, 256:], qo[:, 1024:].T, gw, uw, dw.T,
        lines[0], lines[4, :256], lines[5, :256], lines[1], lines[2], lines[3],
    )
    results, grad_list, saved_list, width_list, head_list = [], [], [], [], []
    for micro in range(micro_count):
        result, record = forward_micro(params, inputs[micro], segment_ids[micro])
        grad_inputs, saved, width_gains, head_gains = backward_micro(
            params, inputs[micro], record, upstream[micro]
        )
        results.append(result.astype(BF))
        grad_list.append(grad_inputs)
        saved_list.append(saved)
        width_list.append(width_gains)
        head_list.append(head_gains)
    (
        h_first, grad_qraw, grad_kraw, grad_values, context, grad_attn,
        h_second, grad_gate, grad_up, hidden, grad_mixed,
    ) = (jnp.concatenate([saved[field] for saved in saved_list], axis=0) for field in range(11))

    def outer(left, right):
        return jnp.einsum("td,tq->dq", left, right, preferred_element_type=F32).astype(BF)

    qo_grad = jnp.concatenate([outer(h_first, grad_qraw), outer(grad_attn, context)], axis=1)
    kv_grad = outer(h_first, jnp.concatenate([grad_kraw, grad_values], axis=1))
    grads = (qo_grad, outer(h_second, grad_gate), outer(h_second, grad_up), outer(grad_mixed, hidden))
    width_sum = [sum(parts) for parts in zip(*width_list)]
    head_sum = [jnp.pad(sum(parts), (0, 640 - 256)) for parts in zip(*head_list)]
    grad_lines = jnp.pad(jnp.stack(width_sum + head_sum), ((0, 2), (0, 0)))
    qg, kg, vg, og, gg, ug, dg, gain_grads = scatter_gradients(
        *(item.reshape(4, 2, 80, 2048) for item in grads), kv_grad, grad_lines
    )
    return (
        jnp.concatenate(results, axis=0),
        jnp.concatenate(grad_list, axis=0),
        qg, kg, vg, og.T, gg, ug, dg.T,
        gain_grads[0, :5], gain_grads[4, :2], gain_grads[5, :2],
        gain_grads[1, :5], gain_grads[2, :5], gain_grads[3, :5],
    )


def solution(mesh):
    in_specs = (
        P("dp", None),
        P("dp", None),
        P("dp", None),
        P("dp", None),
        P("dp", None),
        P("dp", None),
        P(None, "dp"),
        P("dp", None),
        P("dp", None),
        P(None, "dp"),
        P("dp"),
        P("dp"),
        P("dp"),
        P("dp"),
        P("dp"),
        P("dp"),
    )
    out_specs = (
        P("dp", None),
        P("dp", None),
        P("dp", None),
        P("dp", None),
        P("dp", None),
        P(None, "dp"),
        P("dp", None),
        P("dp", None),
        P(None, "dp"),
        P("dp"),
        P("dp"),
        P("dp"),
        P("dp"),
        P("dp"),
        P("dp"),
    )
    return jax.shard_map(
        per_device, mesh=mesh, in_specs=in_specs, out_specs=out_specs, check_vma=False
    )
```

```python
import functools
import math

import jax
import jax.numpy as jnp
from jax import lax
from jax.experimental import pallas as pl
from jax.experimental.pallas import tpu as pltpu
from jax.sharding import PartitionSpec as P

BF = jnp.bfloat16
F32 = jnp.float32
MESH = pl.DeviceIdType.MESH


class Place:
    def __init__(self):
        me = lax.axis_index("dp")
        self.me = me
        self.c = lax.rem(me, 2)
        self.z = lax.rem(lax.div(me, 2), 4)
        self.y = lax.rem(lax.div(me, 8), 4)
        self.x = lax.div(me, 32)
        self.yl = lax.rem(self.y, 2)
        self.yh = lax.div(self.y, 2)
        self.at = {"x": self.x, "y": self.y, "z": self.z}

    def device(self, x, y, z, c):
        return ((x * 4 + y) * 4 + z) * 2 + c

    def moved(self, axis, by):
        return lax.rem(self.at[axis] + by, 4)

    def peer(self, axis, by):
        spot = dict(self.at)
        spot[axis] = self.moved(axis, by)
        return self.device(spot["x"], spot["y"], spot["z"], self.c)

    def sibling(self):
        return self.device(self.x, self.y, self.z, 1 - self.c)

    def group_peers(self):
        found = []
        for dyl in range(2):
            for dz in range(4):
                for dc in range(2):
                    if dyl or dz or dc:
                        yl = lax.rem(self.yl + dyl, 2)
                        z = lax.rem(self.z + dz, 4)
                        c = lax.rem(self.c + dc, 2)
                        found.append(
                            (
                                self.device(self.x, self.yh * 2 + yl, z, c),
                                c * 8 + yl * 4 + z,
                                yl * 8 + z * 2 + c,
                            )
                        )
        return found

    def slot(self):
        return self.c * 8 + self.yl * 4 + self.z

    def natural(self):
        return self.yl * 8 + self.z * 2 + self.c

    def greet(self):
        others = [item[0] for item in self.group_peers()]
        others += [self.peer("x", by) for by in (1, 2, 3)]
        others += [
            self.device(self.x, (1 - self.yh) * 2 + yl, self.z, self.c) for yl in range(2)
        ]
        barrier = pltpu.get_barrier_semaphore()
        for other in others:
            pl.semaphore_signal(barrier, inc=1, device_id=(other,), device_id_type=MESH)
        pl.semaphore_wait(barrier, len(others))


def region(select, half=None):
    index = []
    for axis in "xyz":
        value = select[axis]
        if value is None:
            cut = half is not None
            if axis == "y":
                index += [pl.ds(half, 1) if cut else slice(None), slice(None)]
            else:
                index.append(pl.ds(2 * half, 2) if cut else slice(None))
            half = None
        elif axis == "y":
            index += [lax.div(value, 2), lax.rem(value, 2)]
        else:
            index.append(value)
    return tuple(index)


def half_shape(whole):
    shape, cut = [], True
    for axis in "xyz":
        if axis in whole:
            if axis == "y":
                shape += [1 if cut else 2, 2]
            else:
                shape.append(2 if cut else 4)
            cut = False
    return tuple(shape)


def whole_shape(whole):
    shape = []
    for axis in "xyz":
        if axis in whole:
            shape += [2, 2] if axis == "y" else [4]
    return tuple(shape)


class Sender:
    def __init__(self, send_sems, recv_sems):
        self.send_sems, self.recv_sems = send_sems, recv_sems
        self.used = 0
        self.open = []

    def send(self, source, target, device):
        copy = pltpu.make_async_remote_copy(
            src_ref=source,
            dst_ref=target,
            send_sem=self.send_sems.at[self.used],
            recv_sem=self.recv_sems.at[self.used],
            device_id=(device,),
            device_id_type=MESH,
        )
        self.used += 1
        copy.start()
        self.open.append(copy)
        return copy

    def finish(self):
        for copy in self.open:
            copy.wait_send()
        self.open = []


def gather_class(place, sender, ref, rows, order):
    tail = (pl.ds(rows[0], rows[1]), slice(None))

    def view(select, half=None):
        return ref.at[(place.c,) + region(select, half) + tail]

    def select_for(step, value):
        chosen = {}
        for at, axis in enumerate(order):
            chosen[axis] = None if at < step else value if at == step else place.at[axis]
        return chosen

    def push(part, device):
        return sender.send(part, part, device)

    for step in (0, 1):
        axis = order[step]
        own = view(select_for(step, place.at[axis]))
        sent = [push(own, place.peer(axis, by)) for by in (1, 3, 2)]
        yield
        for copy in sent:
            copy.wait_recv()
    axis = order[2]
    right, left = place.peer(axis, 1), place.peer(axis, 3)
    mine = select_for(2, place.at[axis])
    of_right = select_for(2, place.moved(axis, 1))
    of_left = select_for(2, place.moved(axis, 3))
    of_far = select_for(2, place.moved(axis, 2))
    r0 = push(view(mine, 0), right)
    l1 = push(view(mine, 1), left)
    r1 = push(view(mine, 1), right)
    l0 = push(view(mine, 0), left)
    twin = [push(view(mine), place.sibling())]
    yield
    r0.wait_recv()
    f0 = push(view(of_left, 0), right)
    l1.wait_recv()
    f1 = push(view(of_right, 1), left)
    yield
    r1.wait_recv()
    twin.append(push(view(of_left), place.sibling()))
    l0.wait_recv()
    twin.append(push(view(of_right), place.sibling()))
    yield
    f0.wait_recv()
    twin.append(push(view(of_far, 0), place.sibling()))
    f1.wait_recv()
    twin.append(push(view(of_far, 1), place.sibling()))
    yield
    for copy in twin:
        copy.wait_recv()


GATHER_COPIES = 17
SCATTER_COPIES = 16


def scatter_class(place, sender, ref, twin_ref, landing, rows, order):
    tail = (pl.ds(rows[0], rows[1]), slice(None))
    order = order[::-1]

    def at(select, half=None):
        return (place.c,) + region(select, half) + tail

    def select_for(step, value):
        chosen = {}
        for where, axis in enumerate(order):
            chosen[axis] = (
                place.at[axis] if where < step else value if where == step else None
            )
        return chosen

    def add(index, *others):
        total = ref[index].astype(F32)
        for other in others:
            total = total + other.astype(F32)
        ref[index] = total.astype(BF)

    axis = order[0]
    pieces = []
    for by in (2, 1, 3, 0):
        part = region(select_for(0, place.moved(axis, by))) + tail
        pieces.append(
            (part, sender.send(ref.at[(1 - place.c,) + part], twin_ref.at[part], place.sibling()))
        )
    yield

    def joined(which):
        part, copy = pieces[which]
        copy.wait_recv()
        add((place.c,) + part, twin_ref[part])

    land = landing[0]
    right, left = place.peer(axis, 1), place.peer(axis, 3)
    mine = select_for(0, place.at[axis])
    to_right = select_for(0, place.moved(axis, 1))
    to_left = select_for(0, place.moved(axis, 3))
    far = select_for(0, place.moved(axis, 2))
    joined(0)
    f0 = sender.send(ref.at[at(far, 0)], land.at[0], right)
    f1 = sender.send(ref.at[at(far, 1)], land.at[1], left)
    joined(1)
    r1 = sender.send(ref.at[at(to_right, 1)], land.at[2], right)
    joined(2)
    l0 = sender.send(ref.at[at(to_left, 0)], land.at[3], left)
    joined(3)
    yield
    f0.wait_recv()
    add(at(to_right, 0), land[0])
    r0 = sender.send(ref.at[at(to_right, 0)], land.at[4], right)
    f1.wait_recv()
    add(at(to_left, 1), land[1])
    l1 = sender.send(ref.at[at(to_left, 1)], land.at[5], left)
    yield
    r1.wait_recv()
    l0.wait_recv()
    r0.wait_recv()
    l1.wait_recv()
    add(at(mine, 0), land[4], land[3])
    add(at(mine, 1), land[2], land[5])
    for step in (1, 2):
        axis = order[step]
        land = landing[step]
        sent = [
            sender.send(
                ref.at[at(select_for(step, place.moved(axis, by)))],
                land.at[by - 1],
                place.peer(axis, by),
            )
            for by in (1, 3, 2)
        ]
        yield
        for copy in sent:
            copy.wait_recv()
        add(at(select_for(step, place.at[axis])), land[0], land[1], land[2])


def landing_shapes(rows, order):
    back = order[::-1]
    return [
        pltpu.VMEM((6,) + half_shape(back[1:]) + (rows, 128), BF),
        pltpu.VMEM((3,) + whole_shape(back[2:]) + (rows, 128), BF),
        pltpu.VMEM((3, rows, 128), BF),
    ]


def picker(part, transposed=False):
    i = lax.broadcasted_iota(jnp.int32, (80, 512), 0)
    j = lax.broadcasted_iota(jnp.int32, (80, 512), 1)
    n = lax.shift_right_logical(j, 5)
    r = lax.bitwise_and(j, 7)
    m = lax.bitwise_and(lax.shift_right_logical(j, 3), 3)
    hit = (m == part) & (r < 5) & (i == n * 5 + r)
    return jnp.where(hit, 1.0, 0.0).astype(BF)


def stacked(parts):
    pad = jnp.zeros((3, 128), F32)
    return jnp.concatenate(
        [item for part in parts for item in (part.astype(F32), pad)], axis=0
    )


CLASSES = (
    (0, 0, 32, "xyz"),
    (0, 32, 48, "yzx"),
    (4, 0, 32, "zxy"),
    (1, 0, 80, "xyz"),
    (2, 0, 80, "yzx"),
    (3, 0, 80, "zxy"),
)
BLOCK_ROWS = (80, 80, 80, 80, 32)


def fill_messages(q, o, k, v, g, u, d, gains, msgs, kv_block):
    for slot in range(16):
        lanes = slice(slot * 128, slot * 128 + 128)
        narrow = slice(slot % 8 * 128, slot % 8 * 128 + 128)
        qo = q[:, narrow] if slot < 8 else o[:, narrow]
        msgs[slot] = stacked([g[:, lanes], u[:, lanes], d[:, lanes], qo]).astype(BF)
    flat = stacked([k[:, 0:128], k[:, 128:256], v[:, 0:128], v[:, 128:256]])
    row = lax.broadcasted_iota(jnp.int32, (32, 128), 0)
    for at, target in enumerate(GAIN_ROWS):
        flat = jnp.where(row == target, gains[at : at + 1, :], flat)
    kv_block[...] = flat.astype(BF)


GAIN_ROWS = (5, 13, 21, 29, 6, 14)


def spread_rows(buf, row):
    takes = []
    for x in range(4):
        for yh in range(2):
            for yl in range(2):
                both = [
                    jnp.concatenate(
                        [buf[c, x, yh, yl, z, row // 8 * 8 : row // 8 * 8 + 8, :] for c in range(2)], 0
                    )
                    for z in range(4)
                ]
                takes += both
    every = jnp.concatenate(takes, axis=0)
    i = lax.broadcasted_iota(jnp.int32, (128, 1024), 0)
    j = lax.broadcasted_iota(jnp.int32, (128, 1024), 1)
    pick = jnp.where(j == i * 8 + row % 8, 1.0, 0.0).astype(BF)
    return jnp.dot(pick, every, preferred_element_type=F32)


def gain_line(buf, row, each, width):
    held = spread_rows(buf, row)
    count = lax.broadcasted_iota(jnp.int32, (128, width), 0)
    lane = lax.broadcasted_iota(jnp.int32, (128, width), 1)
    place_in = lane - count * each
    r = lax.broadcasted_iota(jnp.int32, (128, width), 0)
    rep = jnp.where(lax.rem(lane, each) == r, 1.0, 0.0).astype(BF)
    lined = jnp.dot(held.astype(BF), rep, preferred_element_type=F32)
    lined = jnp.where((place_in >= 0) & (place_in < each), lined, 0.0)
    return jnp.sum(lined, axis=0, keepdims=True)


def exchange_start(place, sender, msgs, recv):
    return [
        sender.send(msgs.at[slot], recv.at[place.natural()], device)
        for device, slot, _ in place.group_peers()
    ]


def exchange_take(place, copies, msgs, recv, bufs, kv_block):
    recv[place.natural()] = msgs[place.slot()]
    spot = (place.c, place.x, place.yh, place.yl, place.z)
    bufs[4][spot] = kv_block[...]
    for copy in copies:
        copy.wait_recv()
    flat = recv[...].reshape(512, 128)
    for part, buf in ((3, bufs[0]), (0, bufs[1]), (1, bufs[2]), (2, bufs[3])):
        buf[spot] = jnp.dot(picker(part), flat, preferred_element_type=F32).astype(BF)


def spread_gain(line, each):
    width = line.shape[1]
    count = lax.broadcasted_iota(jnp.int32, (128, width), 0)
    lane = lax.broadcasted_iota(jnp.int32, (128, width), 1)
    inside = lane - count * each
    kept = jnp.where((inside >= 0) & (inside < each), jnp.broadcast_to(line, (128, width)), 0.0)
    r = lax.broadcasted_iota(jnp.int32, (width, 128), 0)
    to = lax.broadcasted_iota(jnp.int32, (width, 128), 1)
    pick = jnp.where(lax.rem(r, each) == to, 1.0, 0.0).astype(BF)
    return jnp.dot(kept.astype(BF), pick, preferred_element_type=F32)


def fill_kv_gradient(kv, gain_lines, buf):
    gains = [spread_gain(line, 5 if at < 4 else 2) for at, line in enumerate(gain_lines)]
    row = lax.broadcasted_iota(jnp.int32, (512, 128), 0)
    seat = lax.bitwise_and(row, 31)
    n = lax.broadcasted_iota(jnp.int32, (512, 16), 0)
    m = lax.broadcasted_iota(jnp.int32, (512, 16), 1)
    repeat = jnp.where(lax.shift_right_logical(n, 5) == m, 1.0, 0.0).astype(BF)
    for group in range(8):
        flat = jnp.zeros((512, 128), F32)
        for part in range(4):
            flat = flat + lax.dot_general(
                picker(part), kv(group, part), (((0,), (0,)), ((), ())), preferred_element_type=F32
            )
        for at, target in enumerate(GAIN_ROWS):
            own = gains[at][group * 16 : group * 16 + 16].astype(BF)
            flat = jnp.where(
                seat == target, jnp.dot(repeat, own, preferred_element_type=F32), flat
            )
        flat = flat.astype(BF)
        for n16 in range(16):
            yl, z, c = n16 // 8, n16 // 2 % 4, n16 % 2
            buf[c, group // 2, group % 2, yl, z] = flat[n16 * 32 : n16 * 32 + 32]


def exchange_out(place, sender, msgs, recv, bufs):
    spot = (place.c, place.x, place.yh, place.yl, place.z)
    flat = jnp.zeros((512, 128), F32)
    for part, buf in ((3, bufs[0]), (0, bufs[1]), (1, bufs[2]), (2, bufs[3])):
        flat = flat + lax.dot_general(
            picker(part), buf[spot], (((0,), (0,)), ((), ())), preferred_element_type=F32
        )
    msgs[...] = flat.astype(BF).reshape(16, 32, 128)
    copies = [
        sender.send(msgs.at[natural], recv.at[place.slot()], device)
        for device, _, natural in place.group_peers()
    ]
    recv[place.slot()] = msgs[place.natural()]
    for copy in copies:
        copy.wait_recv()


NORM_EPS = 1e-06
ROPE_BASE = 1000000.0
MASKED = -1e30
ROWS = 96
PACKS = 2
HEADS = 4


def matmul(left, right):
    return jnp.dot(left, right, preferred_element_type=F32)


def matmul_t(left, right):
    return lax.dot_general(left, right, (((1,), (1,)), ((), ())), preferred_element_type=F32)


def t_matmul(left, right):
    return lax.dot_general(left, right, (((0,), (0,)), ((), ())), preferred_element_type=F32)


def inverse_rms(v):
    return lax.rsqrt(jnp.mean(v * v, axis=-1, keepdims=True) + NORM_EPS)


def rms_back(v, gain, dy):
    r = inverse_rms(v)
    n = v * r
    dg = dy * gain
    dv = r * (dg - n * jnp.mean(dg * n, axis=-1, keepdims=True))
    return dv, jnp.sum(dy * n, axis=0, keepdims=True)


def turn(v, cosine, sine):
    first, second = v[:, 0:128], v[:, 128:256]
    return jnp.concatenate(
        [first * cosine - second * sine, second * cosine + first * sine], axis=1
    )


def spot_of(t):
    return lax.div(t, 4), lax.rem(lax.div(t, 2), 2), lax.rem(t, 2) * 2


def read_tile(buf, t):
    c, yl, z = spot_of(t)
    return jnp.concatenate(
        [buf[c, :, :, yl, z + k].reshape(640, 128) for k in range(2)], axis=1
    )


def write_tile(buf, t, value):
    c, yl, z = spot_of(t)
    value = value.astype(BF)
    for k in range(2):
        buf[c, :, :, yl, z + k] = value[:, k * 128 : k * 128 + 128].reshape(4, 2, 80, 128)


def read_kv(buf, scratch):
    def group(g, carry):
        x, yh = lax.div(g, 2), lax.rem(g, 2)
        blocks = [buf[c, x, yh, yl, z] for yl in range(2) for z in range(4) for c in range(2)]
        flat = jnp.concatenate(blocks, axis=0)
        rows = pl.ds(pl.multiple_of(g * 80, 16), 80)
        for part in range(4):
            scratch[rows, part * 128 : part * 128 + 128] = matmul(picker(part), flat).astype(BF)
        return carry

    lax.fori_loop(0, 8, group, 0)


def tick(tasks):
    for task in list(tasks):
        try:
            next(task)
        except StopIteration:
            tasks.remove(task)


def drain(tasks):
    while tasks:
        tick(tasks)


def layer_kernel(
    tokens, segments, cotangent, q, k, v, o, g, u, d, gains,
    layer_out, grad_tokens, part_out, kv_out,
    *scratch,
):
    weights, grads, twins = scratch[0:5], scratch[5:10], scratch[10:15]
    scratch = scratch[15:]
    landings, scratch = scratch[: 3 * len(CLASSES)], scratch[3 * len(CLASSES) :]
    (
        msgs, recv, msgs_back, recv_back, kv_block, kv_weight, lines,
        h1_s, qraw_s, kraw_s, qf_s, kf_s, vb_s, prob_s, ctx_s, attn_s, x1_s, h2_s,
        slope_s, gelu_s, hidden_s, mixed_s, dm_s, dh2_s, dx1_s, da_s, dctx_s, dq_s, dkv_s,
        cos_s, sin_s, h2t_s, dmt_s,
        send_sems, recv_sems,
    ) = scratch
    place = Place()
    fill_messages(q, o, k, v, g, u, d, gains, msgs, kv_block)
    place.greet()
    sender = Sender(send_sems, recv_sems)
    arrivals = exchange_start(place, sender, msgs, recv)

    t_of = lax.broadcasted_iota(jnp.int32, (ROWS, ROWS), 0)
    u_of = lax.broadcasted_iota(jnp.int32, (ROWS, ROWS), 1)
    lane = lax.broadcasted_iota(jnp.int32, (1, 128), 1).astype(F32)
    frequency = jnp.exp(-math.log(ROPE_BASE) * 2.0 * lane / 256.0)
    allowed = []
    for b in range(PACKS):
        row = jnp.broadcast_to(segments[b : b + 1, :].astype(F32), (ROWS, ROWS))
        same = row == row.T
        earlier = jnp.where(same & (u_of < t_of), 1.0, 0.0)
        angles = jnp.sum(earlier, axis=1, keepdims=True) * frequency
        cos_s[b * ROWS : b * ROWS + ROWS] = jnp.cos(angles)
        sin_s[b * ROWS : b * ROWS + ROWS] = jnp.sin(angles)
        allowed.append(same & (u_of <= t_of))

    exchange_take(place, arrivals, msgs, recv, weights, kv_block)

    def gather(at):
        which, first, count, order = CLASSES[at]
        return gather_class(place, sender, weights[which], (first, count), order)

    near, wide = [gather(at) for at in range(3)], [gather(at) for at in range(3, 6)]
    while near:
        tick(near)
        tick(wide)

    read_kv(weights[4], kv_weight)
    lines[...] = jnp.zeros((8, 640), F32)
    for at, row in enumerate(GAIN_ROWS):
        if at < 4:
            lines[at : at + 1, :] = gain_line(weights[4], row, 5, 640)
        else:
            lines[at : at + 1, 0:256] = gain_line(weights[4], row, 2, 256)
    input_gain, post_attn_gain = lines[0:1, :], lines[1:2, :]
    pre_ffn_gain, post_ffn_gain = lines[2:3, :], lines[3:4, :]
    query_gain, key_gain = lines[4:5, 0:256], lines[5:6, 0:256]
    tick(wide)

    x = tokens[...].astype(F32)
    h1_s[...] = (x * inverse_rms(x) * input_gain).astype(BF)
    cosine, sine = cos_s[...], sin_s[...]
    h1 = h1_s[...]
    for h in range(HEADS):
        raw = matmul(h1, read_tile(weights[0], h))
        qraw_s[h] = raw
        query = turn(raw * inverse_rms(raw) * query_gain, cosine, sine) * (1.0 / 16.0)
        for b in range(PACKS):
            qf_s[b, h * ROWS : h * ROWS + ROWS] = query[b * ROWS : b * ROWS + ROWS].astype(BF)
    tick(wide)
    raw = matmul(h1, kv_weight[:, 0:256])
    kraw_s[...] = raw
    kf_s[...] = turn(raw * inverse_rms(raw) * key_gain, cosine, sine).astype(BF)
    vb_s[...] = matmul(h1, kv_weight[:, 256:512]).astype(BF)
    for b in range(PACKS):
        mine = slice(b * ROWS, b * ROWS + ROWS)
        scores = matmul_t(qf_s[b], kf_s[mine])
        scores = jnp.where(jnp.concatenate([allowed[b]] * HEADS, axis=0), scores, MASKED)
        grown = jnp.exp(scores - jnp.max(scores, axis=-1, keepdims=True))
        prob = grown / jnp.sum(grown, axis=-1, keepdims=True)
        prob_s[b] = prob
        context = matmul(prob.astype(BF), vb_s[mine]).astype(BF)
        for h in range(HEADS):
            ctx_s[h, mine] = context[h * ROWS : h * ROWS + ROWS]
    tick(wide)
    attn = matmul_t(ctx_s[0], read_tile(weights[0], 4))
    for h in range(1, HEADS):
        attn = attn + matmul_t(ctx_s[h], read_tile(weights[0], 4 + h))
    attn_s[...] = attn
    x1 = x + attn * inverse_rms(attn) * post_attn_gain
    x1_s[...] = x1
    h2_s[...] = (x1 * inverse_rms(x1) * pre_ffn_gain).astype(BF)
    h2t_s[...] = h2_s[...].astype(F32).T.astype(BF)
    tick(wide)
    drain(wide)

    mixed_s[...] = jnp.zeros((PACKS * ROWS, 640), F32)

    def feed(t, carry):
        h2 = h2_s[...]
        gate = matmul(h2, read_tile(weights[1], t))
        up = matmul(h2, read_tile(weights[2], t))
        rate = math.sqrt(2.0 / math.pi)
        square = gate * gate
        bent = jnp.tanh(rate * gate * (1.0 + 0.044715 * square))
        half = 0.5 * (1.0 + bent)
        gelu = gate * half
        slope = half + 0.5 * gate * (1.0 - bent * bent) * rate * (1.0 + 3 * 0.044715 * square)
        gelu_s[t] = gelu
        slope_s[t] = up * slope
        hidden = (gelu * up).astype(BF)
        hidden_s[t] = hidden
        mixed_s[...] += matmul_t(hidden, read_tile(weights[3], t))
        return carry

    lax.fori_loop(0, 8, feed, 0)

    c = cotangent[...].astype(F32)
    mixed = mixed_s[...]
    layer_out[...] = (x1_s[...] + mixed * inverse_rms(mixed) * post_ffn_gain).astype(BF)
    dm, post_ffn_line = rms_back(mixed, post_ffn_gain, c)
    dm_s[...] = dm.astype(BF)
    dmt_s[...] = dm_s[...].astype(F32).T.astype(BF)
    dh2_s[...] = jnp.zeros((PACKS * ROWS, 640), F32)

    def feed_back(t):
        dh = matmul(dm_s[...], read_tile(weights[3], t))
        dgate = (dh * slope_s[t]).astype(BF)
        dup = (dh * gelu_s[t]).astype(BF)
        dh2_s[...] += matmul_t(dgate, read_tile(weights[1], t)) + matmul_t(
            dup, read_tile(weights[2], t)
        )
        write_tile(grads[3], t, matmul(dmt_s[...], hidden_s[t]))
        write_tile(grads[1], t, matmul(h2t_s[...], dgate))
        write_tile(grads[2], t, matmul(h2t_s[...], dup))

    def first_half(i, carry):
        feed_back((1 - place.c) * 4 + i)
        return carry

    def second_half(i, carry):
        feed_back(place.c * 4 + i)
        return carry

    def scatter(at):
        which, first, count, order = CLASSES[at]
        return scatter_class(
            place, sender, grads[which], twins[which], landings[3 * at : 3 * at + 3],
            (first, count), order,
        )

    lax.fori_loop(0, 4, first_half, 0)
    wide = [scatter(at) for at in range(3, 6)]
    tick(wide)
    lax.fori_loop(0, 4, second_half, 0)
    tick(wide)

    dx1_part, pre_ffn_line = rms_back(x1_s[...], pre_ffn_gain, dh2_s[...])
    dx1 = c + dx1_part
    dx1_s[...] = dx1
    da, post_attn_line = rms_back(attn_s[...], post_attn_gain, dx1)
    da_s[...] = da.astype(BF)
    dat = da_s[...].astype(F32).T.astype(BF)
    tick(wide)
    for h in range(HEADS):
        dctx = matmul(da_s[...], read_tile(weights[0], 4 + h)).astype(BF)
        for b in range(PACKS):
            dctx_s[b, h * ROWS : h * ROWS + ROWS] = dctx[b * ROWS : b * ROWS + ROWS]
        write_tile(grads[0], 4 + h, matmul(dat, ctx_s[h]))
    tick(wide)
    query_line = jnp.zeros((1, 256), F32)
    key_line = jnp.zeros((1, 256), F32)
    for b in range(PACKS):
        mine = slice(b * ROWS, b * ROWS + ROWS)
        prob, dctx = prob_s[b], dctx_s[b]
        dp = matmul_t(dctx, vb_s[mine])
        ds = (prob * (dp - jnp.sum(prob * dp, axis=-1, keepdims=True))).astype(BF)
        dkv_s[mine, 256:512] = t_matmul(prob.astype(BF), dctx).astype(BF)
        dqf = matmul(ds, kf_s[mine]) * (1.0 / 16.0)
        dkf = t_matmul(ds, qf_s[b])
        cosine, sine = cos_s[mine, :], sin_s[mine, :]
        for h in range(HEADS):
            dq, line = rms_back(
                qraw_s[h, mine], query_gain, turn(dqf[h * ROWS : h * ROWS + ROWS], cosine, -sine)
            )
            dq_s[h, mine] = dq.astype(BF)
            query_line = query_line + line
        dk, line = rms_back(kraw_s[mine, :], key_gain, turn(dkf, cosine, -sine))
        dkv_s[mine, 0:256] = dk.astype(BF)
        key_line = key_line + line
        tick(wide)
    h1t = h1_s[...].astype(F32).T.astype(BF)
    for h in range(HEADS):
        write_tile(grads[0], h, matmul(h1t, dq_s[h]))
    dkv_weight = matmul(h1t, dkv_s[...]).astype(BF)
    tick(wide)
    dh1 = matmul_t(dkv_s[...], kv_weight[...])
    for h in range(HEADS):
        dh1 = dh1 + matmul_t(dq_s[h], read_tile(weights[0], h))
    x = tokens[...].astype(F32)
    dx, input_line = rms_back(x, input_gain, dh1)
    grad_tokens[...] = dx1_s[...] + dx
    fill_kv_gradient(
        lambda group, part: dkv_weight[group * 80 : group * 80 + 80, part * 128 : part * 128 + 128],
        (input_line, post_attn_line, pre_ffn_line, post_ffn_line, query_line, key_line),
        grads[4],
    )
    near = [scatter(at) for at in range(3)]
    while near or wide:
        tick(near)
        tick(wide)
    exchange_out(place, sender, msgs_back, recv_back, grads)
    part_out[...] = recv_back[...]
    kv_out[...] = grads[4][place.c, place.x, place.yh, place.yl, place.z]
    sender.finish()


def run_layer(tokens, segments, cotangent, q, k, v, o_t, g, u, d_t, gains):
    vm = pl.BlockSpec(memory_space=pltpu.VMEM)
    copies = 30 + (GATHER_COPIES + SCATTER_COPIES) * len(CLASSES)
    rows = PACKS * ROWS
    scratch = [pltpu.VMEM((2, 4, 2, 2, 4, count, 128), BF) for count in BLOCK_ROWS * 2]
    scratch += [pltpu.VMEM((4, 2, 2, 4, count, 128), BF) for count in BLOCK_ROWS]
    for _, _, count, order in CLASSES:
        scratch += landing_shapes(count, order)
    scratch += [pltpu.VMEM((16, 32, 128), BF)] * 4
    scratch += [
        pltpu.VMEM((32, 128), BF),
        pltpu.VMEM((640, 512), BF),
        pltpu.VMEM((8, 640), F32),
        pltpu.VMEM((rows, 640), BF),
        pltpu.VMEM((HEADS, rows, 256), F32),
        pltpu.VMEM((rows, 256), F32),
        pltpu.VMEM((PACKS, HEADS * ROWS, 256), BF),
        pltpu.VMEM((rows, 256), BF),
        pltpu.VMEM((rows, 256), BF),
        pltpu.VMEM((PACKS, HEADS * ROWS, ROWS), F32),
        pltpu.VMEM((HEADS, rows, 256), BF),
        pltpu.VMEM((rows, 640), F32),
        pltpu.VMEM((rows, 640), F32),
        pltpu.VMEM((rows, 640), BF),
        pltpu.VMEM((8, rows, 256), F32),
        pltpu.VMEM((8, rows, 256), F32),
        pltpu.VMEM((8, rows, 256), BF),
        pltpu.VMEM((rows, 640), F32),
        pltpu.VMEM((rows, 640), BF),
        pltpu.VMEM((rows, 640), F32),
        pltpu.VMEM((rows, 640), F32),
        pltpu.VMEM((rows, 640), BF),
        pltpu.VMEM((PACKS, HEADS * ROWS, 256), BF),
        pltpu.VMEM((HEADS, rows, 256), BF),
        pltpu.VMEM((rows, 512), BF),
        pltpu.VMEM((rows, 128), F32),
        pltpu.VMEM((rows, 128), F32),
        pltpu.VMEM((640, rows), BF),
        pltpu.VMEM((640, rows), BF),
        pltpu.SemaphoreType.DMA((copies,)),
        pltpu.SemaphoreType.DMA((copies,)),
    ]
    return pl.pallas_call(
        layer_kernel,
        out_shape=(
            jax.ShapeDtypeStruct((rows, 640), BF),
            jax.ShapeDtypeStruct((rows, 640), F32),
            jax.ShapeDtypeStruct((16, 32, 128), BF),
            jax.ShapeDtypeStruct((32, 128), BF),
        ),
        in_specs=[vm] * 11,
        out_specs=(vm,) * 4,
        scratch_shapes=scratch,
        compiler_params=pltpu.CompilerParams(
            collective_id=0, has_side_effects=True, vmem_limit_bytes=60 << 20
        ),
    )(tokens, segments, cotangent, q, k, v, o_t, g, u, d_t, gains)


def finish_kernel(
    layer, grad, recv, own, layer_out, grad_out,
    q_out, k_out, v_out, o_out, g_out, u_out, d_out, *gain_outs,
):
    layer_out[...] = layer[...]
    grad_out[...] = grad[...]
    for slot in range(16):
        part = recv[slot].astype(F32)
        lanes = slice(slot * 128, slot * 128 + 128)
        narrow = slice(slot % 8 * 128, slot % 8 * 128 + 128)
        g_out[:, lanes] = part[0:5]
        u_out[:, lanes] = part[8:13]
        d_out[:, lanes] = part[16:21]
        (q_out if slot < 8 else o_out)[:, narrow] = part[24:29]
    flat = own[...].astype(F32)
    k_out[:, 0:128] = flat[0:5]
    k_out[:, 128:256] = flat[8:13]
    v_out[:, 0:128] = flat[16:21]
    v_out[:, 128:256] = flat[24:29]
    for out, row in zip(gain_outs, GAIN_ROWS):
        out[...] = flat[row : row + 1, 0 : out.shape[1]]


def finish(layer, grad, recv, own):
    vm = pl.BlockSpec(memory_space=pltpu.VMEM)
    shape = lambda *dims: jax.ShapeDtypeStruct(dims, F32)
    return pl.pallas_call(
        finish_kernel,
        out_shape=(
            jax.ShapeDtypeStruct(layer.shape, BF), shape(*grad.shape),
            shape(5, 1024), shape(5, 256), shape(5, 256), shape(5, 1024),
            shape(5, 2048), shape(5, 2048), shape(5, 2048),
            shape(1, 5), shape(1, 5), shape(1, 5), shape(1, 5), shape(1, 2), shape(1, 2),
        ),
        in_specs=[vm] * 4,
        out_specs=(vm,) * 15,
    )(layer, grad, recv, own)


def per_device(
    tokens,
    segment_ids,
    cotangent,
    query_weight,
    key_weight,
    value_weight,
    out_weight,
    gate_weight,
    up_weight,
    down_weight,
    input_gain,
    query_gain,
    key_gain,
    post_attn_gain,
    pre_ffn_gain,
    post_ffn_gain,
):
    gains = (input_gain, post_attn_gain, pre_ffn_gain, post_ffn_gain, query_gain, key_gain)
    gain_rows = jnp.stack([jnp.pad(item.astype(F32), (0, 128 - item.shape[0])) for item in gains])
    gain_rows = jnp.pad(gain_rows, ((0, 2), (0, 0)))
    layer, grad, recv, own = run_layer(
        tokens, segment_ids, cotangent, query_weight, key_weight, value_weight, out_weight.T,
        gate_weight, up_weight, down_weight.T, gain_rows,
    )
    layer, grad, qg, kg, vg, og, gg, ug, dg, ig, pa, pf, po, qn, kn = finish(layer, grad, recv, own)
    ig, pa, pf, po, qn, kn = (item.reshape(-1) for item in (ig, pa, pf, po, qn, kn))
    return (layer, grad, qg, kg, vg, og.T, gg, ug, dg.T, ig, qn, kn, pa, pf, po)


def solution(mesh):
    in_specs = (
        P("dp", None),
        P("dp", None),
        P("dp", None),
        P("dp", None),
        P("dp", None),
        P("dp", None),
        P(None, "dp"),
        P("dp", None),
        P("dp", None),
        P(None, "dp"),
        P("dp"),
        P("dp"),
        P("dp"),
        P("dp"),
        P("dp"),
        P("dp"),
    )
    out_specs = (
        P("dp", None),
        P("dp", None),
        P("dp", None),
        P("dp", None),
        P("dp", None),
        P(None, "dp"),
        P("dp", None),
        P("dp", None),
        P(None, "dp"),
        P("dp"),
        P("dp"),
        P("dp"),
        P("dp"),
        P("dp"),
        P("dp"),
    )
    return jax.shard_map(
        per_device, mesh=mesh, in_specs=in_specs, out_specs=out_specs, check_vma=False
    )
```

```python
import functools
import math

import jax
import jax.numpy as jnp
from jax import lax
from jax.experimental import pallas as pl
from jax.experimental.pallas import tpu as pltpu
from jax.sharding import PartitionSpec as P

BF = jnp.bfloat16
F32 = jnp.float32
MESH = pl.DeviceIdType.MESH


class Place:
    def __init__(self):
        me = lax.axis_index("dp")
        self.me = me
        self.c = lax.rem(me, 2)
        self.z = lax.rem(lax.div(me, 2), 4)
        self.y = lax.rem(lax.div(me, 8), 4)
        self.x = lax.div(me, 32)
        self.yl = lax.rem(self.y, 2)
        self.yh = lax.div(self.y, 2)
        self.at = {"x": self.x, "y": self.y, "z": self.z}

    def device(self, x, y, z, c):
        return ((x * 4 + y) * 4 + z) * 2 + c

    def moved(self, axis, by):
        return lax.rem(self.at[axis] + by, 4)

    def peer(self, axis, by):
        spot = dict(self.at)
        spot[axis] = self.moved(axis, by)
        return self.device(spot["x"], spot["y"], spot["z"], self.c)

    def sibling(self):
        return self.device(self.x, self.y, self.z, 1 - self.c)

    def group_peers(self):
        found = []
        for dyl in range(2):
            for dz in range(4):
                for dc in range(2):
                    if dyl or dz or dc:
                        yl = lax.rem(self.yl + dyl, 2)
                        z = lax.rem(self.z + dz, 4)
                        c = lax.rem(self.c + dc, 2)
                        found.append(
                            (
                                self.device(self.x, self.yh * 2 + yl, z, c),
                                c * 8 + yl * 4 + z,
                                yl * 8 + z * 2 + c,
                            )
                        )
        return found

    def slot(self):
        return self.c * 8 + self.yl * 4 + self.z

    def natural(self):
        return self.yl * 8 + self.z * 2 + self.c

    def greet(self):
        others = [item[0] for item in self.group_peers()]
        others += [self.peer("x", by) for by in (1, 2, 3)]
        others += [
            self.device(self.x, (1 - self.yh) * 2 + yl, self.z, self.c) for yl in range(2)
        ]
        barrier = pltpu.get_barrier_semaphore()
        for other in others:
            pl.semaphore_signal(barrier, inc=1, device_id=(other,), device_id_type=MESH)
        self.greeted = len(others)

    def await_greetings(self):
        pl.semaphore_wait(pltpu.get_barrier_semaphore(), self.greeted)


def region(select, half=None):
    index = []
    for axis in "xyz":
        value = select[axis]
        if value is None:
            cut = half is not None
            if axis == "y":
                index += [pl.ds(half, 1) if cut else slice(None), slice(None)]
            else:
                index.append(pl.ds(2 * half, 2) if cut else slice(None))
            half = None
        elif axis == "y":
            index += [lax.div(value, 2), lax.rem(value, 2)]
        else:
            index.append(value)
    return tuple(index)


def half_shape(whole):
    shape, cut = [], True
    for axis in "xyz":
        if axis in whole:
            if axis == "y":
                shape += [1 if cut else 2, 2]
            else:
                shape.append(2 if cut else 4)
            cut = False
    return tuple(shape)


def whole_shape(whole):
    shape = []
    for axis in "xyz":
        if axis in whole:
            shape += [2, 2] if axis == "y" else [4]
    return tuple(shape)


class Sender:
    def __init__(self, send_sems, recv_sems):
        self.send_sems, self.recv_sems = send_sems, recv_sems
        self.used = 0
        self.open = []

    def send(self, source, target, device):
        copy = pltpu.make_async_remote_copy(
            src_ref=source,
            dst_ref=target,
            send_sem=self.send_sems.at[self.used],
            recv_sem=self.recv_sems.at[self.used],
            device_id=(device,),
            device_id_type=MESH,
        )
        self.used += 1
        copy.start()
        self.open.append(copy)
        return copy

    def finish(self):
        for copy in self.open:
            copy.wait_send()
        self.open = []


def gather_class(place, sender, ref, rows, order):
    tail = (pl.ds(rows[0], rows[1]), slice(None))

    def view(select, half=None):
        return ref.at[(place.c,) + region(select, half) + tail]

    def select_for(step, value):
        chosen = {}
        for at, axis in enumerate(order):
            chosen[axis] = None if at < step else value if at == step else place.at[axis]
        return chosen

    def push(part, device):
        return sender.send(part, part, device)

    for step in (0, 1):
        axis = order[step]
        own = view(select_for(step, place.at[axis]))
        sent = [push(own, place.peer(axis, by)) for by in (1, 3, 2)]
        yield
        for copy in sent:
            copy.wait_recv()
    axis = order[2]
    right, left = place.peer(axis, 1), place.peer(axis, 3)
    mine = select_for(2, place.at[axis])
    of_right = select_for(2, place.moved(axis, 1))
    of_left = select_for(2, place.moved(axis, 3))
    of_far = select_for(2, place.moved(axis, 2))
    r0 = push(view(mine, 0), right)
    l1 = push(view(mine, 1), left)
    r1 = push(view(mine, 1), right)
    l0 = push(view(mine, 0), left)
    twin = [push(view(mine), place.sibling())]
    yield
    r0.wait_recv()
    f0 = push(view(of_left, 0), right)
    l1.wait_recv()
    f1 = push(view(of_right, 1), left)
    yield
    r1.wait_recv()
    twin.append(push(view(of_left), place.sibling()))
    l0.wait_recv()
    twin.append(push(view(of_right), place.sibling()))
    yield
    f0.wait_recv()
    twin.append(push(view(of_far, 0), place.sibling()))
    f1.wait_recv()
    twin.append(push(view(of_far, 1), place.sibling()))
    yield
    for copy in twin:
        copy.wait_recv()


GATHER_COPIES = 17
SCATTER_COPIES = 16


def scatter_class(place, sender, ref, twin_ref, landing, rows, order):
    tail = (pl.ds(rows[0], rows[1]), slice(None))
    order = order[::-1]

    def at(select, half=None):
        return (place.c,) + region(select, half) + tail

    def select_for(step, value):
        chosen = {}
        for where, axis in enumerate(order):
            chosen[axis] = (
                place.at[axis] if where < step else value if where == step else None
            )
        return chosen

    def add(index, *others):
        total = ref[index].astype(F32)
        for other in others:
            total = total + other.astype(F32)
        ref[index] = total.astype(BF)

    axis = order[0]
    pieces = []
    for by in (2, 1, 3, 0):
        part = region(select_for(0, place.moved(axis, by))) + tail
        pieces.append(
            (part, sender.send(ref.at[(1 - place.c,) + part], twin_ref.at[part], place.sibling()))
        )
    yield

    def joined(which):
        part, copy = pieces[which]
        copy.wait_recv()
        add((place.c,) + part, twin_ref[part])

    land = landing[0]
    right, left = place.peer(axis, 1), place.peer(axis, 3)
    mine = select_for(0, place.at[axis])
    to_right = select_for(0, place.moved(axis, 1))
    to_left = select_for(0, place.moved(axis, 3))
    far = select_for(0, place.moved(axis, 2))
    joined(0)
    f0 = sender.send(ref.at[at(far, 0)], land.at[0], right)
    f1 = sender.send(ref.at[at(far, 1)], land.at[1], left)
    joined(1)
    r1 = sender.send(ref.at[at(to_right, 1)], land.at[2], right)
    joined(2)
    l0 = sender.send(ref.at[at(to_left, 0)], land.at[3], left)
    joined(3)
    yield
    f0.wait_recv()
    add(at(to_right, 0), land[0])
    r0 = sender.send(ref.at[at(to_right, 0)], land.at[4], right)
    f1.wait_recv()
    add(at(to_left, 1), land[1])
    l1 = sender.send(ref.at[at(to_left, 1)], land.at[5], left)
    yield
    r1.wait_recv()
    l0.wait_recv()
    r0.wait_recv()
    l1.wait_recv()
    add(at(mine, 0), land[4], land[3])
    add(at(mine, 1), land[2], land[5])
    for step in (1, 2):
        axis = order[step]
        land = landing[step]
        sent = [
            sender.send(
                ref.at[at(select_for(step, place.moved(axis, by)))],
                land.at[by - 1],
                place.peer(axis, by),
            )
            for by in (1, 3, 2)
        ]
        yield
        for copy in sent:
            copy.wait_recv()
        add(at(select_for(step, place.at[axis])), land[0], land[1], land[2])


def landing_shapes(rows, order):
    back = order[::-1]
    return [
        pltpu.VMEM((6,) + half_shape(back[1:]) + (rows, 128), BF),
        pltpu.VMEM((3,) + whole_shape(back[2:]) + (rows, 128), BF),
        pltpu.VMEM((3, rows, 128), BF),
    ]


GAIN_ROWS = (5, 13, 21, 29, 6, 14)
PICKS = 4 * 80 + 6 * 16


def picks(row, seat):
    n = lax.shift_right_logical(seat, 5)
    inner = lax.bitwise_and(seat, 31)
    r = lax.bitwise_and(seat, 7)
    wanted = jnp.where(r < 5, lax.shift_right_logical(inner, 3) * 80 + n * 5 + r, -1)
    for at, target in enumerate(GAIN_ROWS):
        wanted = jnp.where(inner == target, 320 + at * 16 + n, wanted)
    return jnp.where(wanted == row, 1.0, 0.0).astype(BF)


def fill_picks(pick, pick_t):
    for first in range(0, PICKS, 32):
        shape = (32, 512)
        pick[first : first + 32] = picks(
            lax.broadcasted_iota(jnp.int32, shape, 0) + first, lax.broadcasted_iota(jnp.int32, shape, 1)
        )
    for first in range(0, 512, 32):
        shape = (32, PICKS)
        pick_t[first : first + 32] = picks(
            lax.broadcasted_iota(jnp.int32, shape, 1), lax.broadcasted_iota(jnp.int32, shape, 0) + first
        )


def stacked(parts):
    pad = jnp.zeros((3, 128), F32)
    return jnp.concatenate(
        [item for part in parts for item in (part.astype(F32), pad)], axis=0
    )


CLASSES = (
    (0, 0, 32, "xyz"),
    (0, 32, 48, "yzx"),
    (4, 0, 32, "zxy"),
    (1, 0, 80, "xyz"),
    (2, 0, 80, "yzx"),
    (3, 0, 80, "zxy"),
)
BLOCK_ROWS = (80, 80, 80, 80, 32)


def fill_messages(q, o, k, v, g, u, d, gains, msgs, kv_block):
    for slot in range(16):
        lanes = slice(slot * 128, slot * 128 + 128)
        narrow = slice(slot % 8 * 128, slot % 8 * 128 + 128)
        qo = q[:, narrow] if slot < 8 else o[:, narrow]
        msgs[slot] = stacked([g[:, lanes], u[:, lanes], d[:, lanes], qo]).astype(BF)
    flat = stacked([k[:, 0:128], k[:, 128:256], v[:, 0:128], v[:, 128:256]])
    row = lax.broadcasted_iota(jnp.int32, (32, 128), 0)
    for gain, target in zip(gains, GAIN_ROWS):
        flat = jnp.where(row == target, gain, flat)
    kv_block[...] = flat.astype(BF)


def exchange_start(place, sender, msgs, recv):
    return [
        sender.send(msgs.at[slot], recv.at[place.natural()], device)
        for device, slot, _ in place.group_peers()
    ]


def exchange_take(place, copies, msgs, recv, bufs, kv_block, pick):
    recv[place.natural()] = msgs[place.slot()]
    spot = (place.c, place.x, place.yh, place.yl, place.z)
    bufs[4][spot] = kv_block[...]
    for copy in copies:
        copy.wait_recv()
    flat = matmul(pick[0:320], recv[...].reshape(512, 128)).astype(BF)
    for part, buf in ((3, bufs[0]), (0, bufs[1]), (1, bufs[2]), (2, bufs[3])):
        buf[spot] = flat[part * 80 : part * 80 + 80]


def read_kv(buf, pick, kv_weight, gain_parts):
    def group(g, carry):
        x, yh = lax.div(g, 2), lax.rem(g, 2)
        blocks = [buf[c, x, yh, yl, z] for yl in range(2) for z in range(4) for c in range(2)]
        parts = matmul(pick[...], jnp.concatenate(blocks, axis=0))
        rows = pl.ds(pl.multiple_of(g * 80, 16), 80)
        for part in range(4):
            kv_weight[rows, part * 128 : part * 128 + 128] = parts[
                part * 80 : part * 80 + 80
            ].astype(BF)
        for at in range(6):
            gain_parts[at, pl.ds(pl.multiple_of(g * 16, 16), 16)] = parts[
                320 + at * 16 : 336 + at * 16
            ]
        return carry

    lax.fori_loop(0, 8, group, 0)


def owned(each, width):
    n = lax.broadcasted_iota(jnp.int32, (128, width), 0)
    inside = lax.broadcasted_iota(jnp.int32, (128, width), 1) - n * each
    return (inside >= 0) & (inside < each)


def seats(shape, lane_axis, each):
    lane = lax.broadcasted_iota(jnp.int32, shape, lane_axis)
    r = lax.broadcasted_iota(jnp.int32, shape, 1 - lane_axis)
    return jnp.where(lax.rem(lane, each) == r, 1.0, 0.0).astype(BF)


def read_gains(gain_parts, lines):
    for first, count, each, width in ((0, 4, 5, 640), (4, 2, 2, 256)):
        held = gain_parts[first : first + count].reshape(count * 128, 128).astype(BF)
        spread = matmul(held, seats((128, width), 1, each))
        mine = owned(each, width)
        for at in range(count):
            line = jnp.where(mine, spread[at * 128 : at * 128 + 128], 0.0)
            lines[first + at : first + at + 1, 0:width] = jnp.sum(line, axis=0, keepdims=True)


def fill_kv_gradient(kv, gain_lines, gain_parts, pick_t, buf):
    for at, line in enumerate(gain_lines):
        each, width = (5, 640) if at < 4 else (2, 256)
        kept = jnp.where(owned(each, width), jnp.broadcast_to(line, (128, width)), 0.0)
        gain_parts[at] = matmul(kept.astype(BF), seats((width, 128), 0, each))

    def group(g, carry):
        rows = pl.ds(pl.multiple_of(g * 80, 16), 80)
        parts = [kv[rows, part * 128 : part * 128 + 128] for part in range(4)]
        parts += [gain_parts[at, pl.ds(pl.multiple_of(g * 16, 16), 16)].astype(BF) for at in range(6)]
        flat = matmul(pick_t[...], jnp.concatenate(parts, axis=0)).astype(BF)
        x, yh = lax.div(g, 2), lax.rem(g, 2)
        for n in range(16):
            yl, z, c = n // 8, n // 2 % 4, n % 2
            buf[c, x, yh, yl, z] = flat[n * 32 : n * 32 + 32]
        return carry

    lax.fori_loop(0, 8, group, 0)


def exchange_out(place, sender, msgs, recv, bufs, pick_t):
    spot = (place.c, place.x, place.yh, place.yl, place.z)
    parts = [bufs[1][spot], bufs[2][spot], bufs[3][spot], bufs[0][spot]]
    parts.append(jnp.zeros((PICKS - 320, 128), BF))
    flat = matmul(pick_t[...], jnp.concatenate(parts, axis=0))
    msgs[...] = flat.astype(BF).reshape(16, 32, 128)
    copies = [
        sender.send(msgs.at[natural], recv.at[place.slot()], device)
        for device, _, natural in place.group_peers()
    ]
    recv[place.slot()] = msgs[place.natural()]
    for copy in copies:
        copy.wait_recv()


NORM_EPS = 1e-06
ROPE_BASE = 1000000.0
MASKED = -1e30
ROWS = 96
PACKS = 2
HEADS = 4


def matmul(left, right):
    return jnp.dot(left, right, preferred_element_type=F32)


def matmul_t(left, right):
    return lax.dot_general(left, right, (((1,), (1,)), ((), ())), preferred_element_type=F32)


def t_matmul(left, right):
    return lax.dot_general(left, right, (((0,), (0,)), ((), ())), preferred_element_type=F32)


def inverse_rms(v):
    return lax.rsqrt(jnp.mean(v * v, axis=-1, keepdims=True) + NORM_EPS)


def rms_back(v, gain, dy):
    r = inverse_rms(v)
    n = v * r
    dg = dy * gain
    dv = r * (dg - n * jnp.mean(dg * n, axis=-1, keepdims=True))
    return dv, jnp.sum(dy * n, axis=0, keepdims=True)


def turn(v, cosine, sine):
    first, second = v[:, 0:128], v[:, 128:256]
    return jnp.concatenate(
        [first * cosine - second * sine, second * cosine + first * sine], axis=1
    )


def spot_of(t):
    return lax.div(t, 4), lax.rem(lax.div(t, 2), 2), lax.rem(t, 2) * 2


def read_tile(buf, t):
    c, yl, z = spot_of(t)
    return jnp.concatenate(
        [buf[c, :, :, yl, z + k].reshape(640, 128) for k in range(2)], axis=1
    )


def write_tile(buf, t, value):
    c, yl, z = spot_of(t)
    value = value.astype(BF)
    for k in range(2):
        buf[c, :, :, yl, z + k] = value[:, k * 128 : k * 128 + 128].reshape(4, 2, 80, 128)


def tick(tasks):
    for task in list(tasks):
        try:
            next(task)
        except StopIteration:
            tasks.remove(task)


def drain(tasks):
    while tasks:
        tick(tasks)


def layer_kernel(
    tokens, segments, cotangent, q, k, v, o, g, u, d,
    input_gain, post_attn_gain, pre_ffn_gain, post_ffn_gain, query_gain, key_gain,
    layer_out, grad_tokens, part_out, kv_out,
    *scratch,
):
    weights, grads, twins = scratch[0:5], scratch[5:10], scratch[10:15]
    scratch = scratch[15:]
    landings, scratch = scratch[: 3 * len(CLASSES)], scratch[3 * len(CLASSES) :]
    (
        msgs, recv, msgs_back, recv_back, kv_block, kv_weight, kv_weight_grad, lines,
        h1_s, qraw_s, kraw_s, qf_s, kf_s, vb_s, prob_s, ctx_s, attn_s, x1_s, h2_s,
        slope_s, gelu_s, hidden_s, mixed_s, dm_s, dh2_s, dx1_s, da_s, dctx_s, dq_s, dkv_s,
        cos_s, sin_s, h2t_s, dmt_s, gain_parts, pick, pick_t,
        send_sems, recv_sems,
    ) = scratch
    place = Place()
    place.greet()
    gains = (input_gain, post_attn_gain, pre_ffn_gain, post_ffn_gain, query_gain, key_gain)
    gains = [jnp.pad(item[...].astype(F32)[None, :], ((0, 0), (0, 128 - item.shape[0]))) for item in gains]
    fill_messages(q, o, k, v, g, u, d, gains, msgs, kv_block)
    fill_picks(pick, pick_t)
    sender = Sender(send_sems, recv_sems)
    place.await_greetings()
    arrivals = exchange_start(place, sender, msgs, recv)

    t_of = lax.broadcasted_iota(jnp.int32, (ROWS, ROWS), 0)
    u_of = lax.broadcasted_iota(jnp.int32, (ROWS, ROWS), 1)
    lane = lax.broadcasted_iota(jnp.int32, (1, 128), 1).astype(F32)
    frequency = jnp.exp(-math.log(ROPE_BASE) * 2.0 * lane / 256.0)
    allowed = []
    for b in range(PACKS):
        row = jnp.broadcast_to(segments[b : b + 1, :].astype(F32), (ROWS, ROWS))
        same = row == row.T
        earlier = jnp.where(same & (u_of < t_of), 1.0, 0.0)
        angles = jnp.sum(earlier, axis=1, keepdims=True) * frequency
        cos_s[b * ROWS : b * ROWS + ROWS] = jnp.cos(angles)
        sin_s[b * ROWS : b * ROWS + ROWS] = jnp.sin(angles)
        allowed.append(same & (u_of <= t_of))

    exchange_take(place, arrivals, msgs, recv, weights, kv_block, pick)

    def gather(at):
        which, first, count, order = CLASSES[at]
        return gather_class(place, sender, weights[which], (first, count), order)

    near, wide = [gather(at) for at in range(3)], [gather(at) for at in range(3, 6)]
    tick(near)
    tick(wide)
    tick(near)
    tick(wide)
    tick(near)
    tick(near)
    tick(wide)
    tick(near)
    tick(near)
    tick(near)
    tick(wide)
    read_kv(weights[4], pick, kv_weight, gain_parts)
    read_gains(gain_parts, lines)
    input_gain, post_attn_gain = lines[0:1, :], lines[1:2, :]
    pre_ffn_gain, post_ffn_gain = lines[2:3, :], lines[3:4, :]
    query_gain, key_gain = lines[4:5, 0:256], lines[5:6, 0:256]

    x = tokens[...].astype(F32)
    h1_s[...] = (x * inverse_rms(x) * input_gain).astype(BF)
    cosine, sine = cos_s[...], sin_s[...]
    h1 = h1_s[...]
    for h in range(HEADS):
        raw = matmul(h1, read_tile(weights[0], h))
        qraw_s[h] = raw
        query = turn(raw * inverse_rms(raw) * query_gain, cosine, sine) * (1.0 / 16.0)
        for b in range(PACKS):
            qf_s[b, h * ROWS : h * ROWS + ROWS] = query[b * ROWS : b * ROWS + ROWS].astype(BF)
    tick(wide)
    raw = matmul(h1, kv_weight[:, 0:256])
    kraw_s[...] = raw
    kf_s[...] = turn(raw * inverse_rms(raw) * key_gain, cosine, sine).astype(BF)
    vb_s[...] = matmul(h1, kv_weight[:, 256:512]).astype(BF)
    for b in range(PACKS):
        mine = slice(b * ROWS, b * ROWS + ROWS)
        scores = matmul_t(qf_s[b], kf_s[mine])
        scores = jnp.where(jnp.concatenate([allowed[b]] * HEADS, axis=0), scores, MASKED)
        grown = jnp.exp(scores - jnp.max(scores, axis=-1, keepdims=True))
        prob = grown / jnp.sum(grown, axis=-1, keepdims=True)
        prob_s[b] = prob
        context = matmul(prob.astype(BF), vb_s[mine]).astype(BF)
        for h in range(HEADS):
            ctx_s[h, mine] = context[h * ROWS : h * ROWS + ROWS]
    tick(wide)
    attn = matmul_t(ctx_s[0], read_tile(weights[0], 4))
    for h in range(1, HEADS):
        attn = attn + matmul_t(ctx_s[h], read_tile(weights[0], 4 + h))
    attn_s[...] = attn
    x1 = x + attn * inverse_rms(attn) * post_attn_gain
    x1_s[...] = x1
    h2_s[...] = (x1 * inverse_rms(x1) * pre_ffn_gain).astype(BF)
    h2t_s[...] = h2_s[...].astype(F32).T.astype(BF)
    tick(wide)
    drain(wide)

    mixed_s[...] = jnp.zeros((PACKS * ROWS, 640), F32)

    def feed(t, carry):
        h2 = h2_s[...]
        gate = matmul(h2, read_tile(weights[1], t))
        up = matmul(h2, read_tile(weights[2], t))
        rate = math.sqrt(2.0 / math.pi)
        square = gate * gate
        bent = jnp.tanh(rate * gate * (1.0 + 0.044715 * square))
        half = 0.5 * (1.0 + bent)
        gelu = gate * half
        slope = half + 0.5 * gate * (1.0 - bent * bent) * rate * (1.0 + 3 * 0.044715 * square)
        gelu_s[t] = gelu
        slope_s[t] = up * slope
        hidden = (gelu * up).astype(BF)
        hidden_s[t] = hidden
        mixed_s[...] += matmul_t(hidden, read_tile(weights[3], t))
        return carry

    lax.fori_loop(0, 8, feed, 0)

    c = cotangent[...].astype(F32)
    mixed = mixed_s[...]
    layer_out[...] = (x1_s[...] + mixed * inverse_rms(mixed) * post_ffn_gain).astype(BF)
    dm, post_ffn_line = rms_back(mixed, post_ffn_gain, c)
    dm_s[...] = dm.astype(BF)
    dmt_s[...] = dm_s[...].astype(F32).T.astype(BF)
    dh2_s[...] = jnp.zeros((PACKS * ROWS, 640), F32)

    def feed_back(t):
        dh = matmul(dm_s[...], read_tile(weights[3], t))
        dgate = (dh * slope_s[t]).astype(BF)
        dup = (dh * gelu_s[t]).astype(BF)
        dh2_s[...] += matmul_t(dgate, read_tile(weights[1], t)) + matmul_t(
            dup, read_tile(weights[2], t)
        )
        write_tile(grads[3], t, matmul(dmt_s[...], hidden_s[t]))
        write_tile(grads[1], t, matmul(h2t_s[...], dgate))
        write_tile(grads[2], t, matmul(h2t_s[...], dup))

    def first_half(i, carry):
        feed_back((1 - place.c) * 4 + i)
        return carry

    def second_half(i, carry):
        feed_back(place.c * 4 + i)
        return carry

    def scatter(at):
        which, first, count, order = CLASSES[at]
        return scatter_class(
            place, sender, grads[which], twins[which], landings[3 * at : 3 * at + 3],
            (first, count), order,
        )

    lax.fori_loop(0, 4, first_half, 0)
    wide = [scatter(at) for at in range(3, 6)]
    tick(wide)
    lax.fori_loop(0, 4, second_half, 0)
    tick(wide)

    dx1_part, pre_ffn_line = rms_back(x1_s[...], pre_ffn_gain, dh2_s[...])
    dx1 = c + dx1_part
    dx1_s[...] = dx1
    da, post_attn_line = rms_back(attn_s[...], post_attn_gain, dx1)
    da_s[...] = da.astype(BF)
    dat = da_s[...].astype(F32).T.astype(BF)
    for h in range(HEADS):
        dctx = matmul(da_s[...], read_tile(weights[0], 4 + h)).astype(BF)
        for b in range(PACKS):
            dctx_s[b, h * ROWS : h * ROWS + ROWS] = dctx[b * ROWS : b * ROWS + ROWS]
        write_tile(grads[0], 4 + h, matmul(dat, ctx_s[h]))
    query_line = jnp.zeros((1, 256), F32)
    key_line = jnp.zeros((1, 256), F32)
    for b in range(PACKS):
        mine = slice(b * ROWS, b * ROWS + ROWS)
        prob, dctx = prob_s[b], dctx_s[b]
        dp = matmul_t(dctx, vb_s[mine])
        ds = (prob * (dp - jnp.sum(prob * dp, axis=-1, keepdims=True))).astype(BF)
        dkv_s[mine, 256:512] = t_matmul(prob.astype(BF), dctx).astype(BF)
        dqf = matmul(ds, kf_s[mine]) * (1.0 / 16.0)
        dkf = t_matmul(ds, qf_s[b])
        cosine, sine = cos_s[mine, :], sin_s[mine, :]
        for h in range(HEADS):
            dq, line = rms_back(
                qraw_s[h, mine], query_gain, turn(dqf[h * ROWS : h * ROWS + ROWS], cosine, -sine)
            )
            dq_s[h, mine] = dq.astype(BF)
            query_line = query_line + line
        dk, line = rms_back(kraw_s[mine, :], key_gain, turn(dkf, cosine, -sine))
        dkv_s[mine, 0:256] = dk.astype(BF)
        key_line = key_line + line
    tick(wide)
    h1t = h1_s[...].astype(F32).T.astype(BF)
    for h in range(HEADS):
        write_tile(grads[0], h, matmul(h1t, dq_s[h]))
    near = [scatter(at) for at in range(2)]
    tick(near)
    kv_weight_grad[...] = matmul(h1t, dkv_s[...]).astype(BF)
    dh1 = matmul_t(dkv_s[...], kv_weight[...])
    for h in range(HEADS):
        dh1 = dh1 + matmul_t(dq_s[h], read_tile(weights[0], h))
    x = tokens[...].astype(F32)
    dx, input_line = rms_back(x, input_gain, dh1)
    fill_kv_gradient(
        kv_weight_grad,
        (input_line, post_attn_line, pre_ffn_line, post_ffn_line, query_line, key_line),
        gain_parts, pick_t, grads[4],
    )
    last = [scatter(2)]
    tick(last)
    tick(near)
    tick(last)
    near = near + last
    grad_tokens[...] = dx1_s[...] + dx
    while near or wide:
        tick(wide)
        tick(near)
    exchange_out(place, sender, msgs_back, recv_back, grads, pick_t)
    part_out[...] = recv_back[...]
    kv_out[...] = grads[4][place.c, place.x, place.yh, place.yl, place.z]
    sender.finish()


def run_layer(tokens, segments, cotangent, q, k, v, o_t, g, u, d_t, *gains):
    vm = pl.BlockSpec(memory_space=pltpu.VMEM)
    copies = 30 + (GATHER_COPIES + SCATTER_COPIES) * len(CLASSES)
    rows = PACKS * ROWS
    scratch = [pltpu.VMEM((2, 4, 2, 2, 4, count, 128), BF) for count in BLOCK_ROWS * 2]
    scratch += [pltpu.VMEM((4, 2, 2, 4, count, 128), BF) for count in BLOCK_ROWS]
    for _, _, count, order in CLASSES:
        scratch += landing_shapes(count, order)
    scratch += [pltpu.VMEM((16, 32, 128), BF)] * 4
    scratch += [
        pltpu.VMEM((32, 128), BF),
        pltpu.VMEM((640, 512), BF),
        pltpu.VMEM((640, 512), BF),
        pltpu.VMEM((8, 640), F32),
        pltpu.VMEM((rows, 640), BF),
        pltpu.VMEM((HEADS, rows, 256), F32),
        pltpu.VMEM((rows, 256), F32),
        pltpu.VMEM((PACKS, HEADS * ROWS, 256), BF),
        pltpu.VMEM((rows, 256), BF),
        pltpu.VMEM((rows, 256), BF),
        pltpu.VMEM((PACKS, HEADS * ROWS, ROWS), F32),
        pltpu.VMEM((HEADS, rows, 256), BF),
        pltpu.VMEM((rows, 640), F32),
        pltpu.VMEM((rows, 640), F32),
        pltpu.VMEM((rows, 640), BF),
        pltpu.VMEM((8, rows, 256), F32),
        pltpu.VMEM((8, rows, 256), F32),
        pltpu.VMEM((8, rows, 256), BF),
        pltpu.VMEM((rows, 640), F32),
        pltpu.VMEM((rows, 640), BF),
        pltpu.VMEM((rows, 640), F32),
        pltpu.VMEM((rows, 640), F32),
        pltpu.VMEM((rows, 640), BF),
        pltpu.VMEM((PACKS, HEADS * ROWS, 256), BF),
        pltpu.VMEM((HEADS, rows, 256), BF),
        pltpu.VMEM((rows, 512), BF),
        pltpu.VMEM((rows, 128), F32),
        pltpu.VMEM((rows, 128), F32),
        pltpu.VMEM((640, rows), BF),
        pltpu.VMEM((640, rows), BF),
        pltpu.VMEM((6, 128, 128), F32),
        pltpu.VMEM((PICKS, 512), BF),
        pltpu.VMEM((512, PICKS), BF),
        pltpu.SemaphoreType.DMA((copies,)),
        pltpu.SemaphoreType.DMA((copies,)),
    ]
    return pl.pallas_call(
        layer_kernel,
        out_shape=(
            jax.ShapeDtypeStruct((rows, 640), BF),
            jax.ShapeDtypeStruct((rows, 640), F32),
            jax.ShapeDtypeStruct((16, 32, 128), BF),
            jax.ShapeDtypeStruct((32, 128), BF),
        ),
        in_specs=[vm] * 16,
        out_specs=(vm,) * 4,
        scratch_shapes=scratch,
        compiler_params=pltpu.CompilerParams(
            collective_id=0, has_side_effects=True, vmem_limit_bytes=60 << 20
        ),
    )(tokens, segments, cotangent, q, k, v, o_t, g, u, d_t, *gains)


def finish_kernel(
    layer, grad, recv, own, layer_out, grad_out,
    q_out, k_out, v_out, o_out, g_out, u_out, d_out, *gain_outs,
):
    layer_out[...] = layer[...]
    grad_out[...] = grad[...]
    for slot in range(16):
        part = recv[slot].astype(F32)
        lanes = slice(slot * 128, slot * 128 + 128)
        narrow = slice(slot % 8 * 128, slot % 8 * 128 + 128)
        g_out[:, lanes] = part[0:5]
        u_out[:, lanes] = part[8:13]
        d_out[:, lanes] = part[16:21]
        (q_out if slot < 8 else o_out)[:, narrow] = part[24:29]
    flat = own[...].astype(F32)
    k_out[:, 0:128] = flat[0:5]
    k_out[:, 128:256] = flat[8:13]
    v_out[:, 0:128] = flat[16:21]
    v_out[:, 128:256] = flat[24:29]
    for out, row in zip(gain_outs, GAIN_ROWS):
        out[...] = flat[row : row + 1, 0 : out.shape[1]]


def finish(layer, grad, recv, own):
    vm = pl.BlockSpec(memory_space=pltpu.VMEM)
    shape = lambda *dims: jax.ShapeDtypeStruct(dims, F32)
    return pl.pallas_call(
        finish_kernel,
        out_shape=(
            jax.ShapeDtypeStruct(layer.shape, BF), shape(*grad.shape),
            shape(5, 1024), shape(5, 256), shape(5, 256), shape(5, 1024),
            shape(5, 2048), shape(5, 2048), shape(5, 2048),
            shape(1, 5), shape(1, 5), shape(1, 5), shape(1, 5), shape(1, 2), shape(1, 2),
        ),
        in_specs=[vm] * 4,
        out_specs=(vm,) * 15,
    )(layer, grad, recv, own)


def per_device(
    tokens,
    segment_ids,
    cotangent,
    query_weight,
    key_weight,
    value_weight,
    out_weight,
    gate_weight,
    up_weight,
    down_weight,
    input_gain,
    query_gain,
    key_gain,
    post_attn_gain,
    pre_ffn_gain,
    post_ffn_gain,
):
    layer, grad, recv, own = run_layer(
        tokens, segment_ids, cotangent, query_weight, key_weight, value_weight, out_weight.T,
        gate_weight, up_weight, down_weight.T,
        input_gain, post_attn_gain, pre_ffn_gain, post_ffn_gain, query_gain, key_gain,
    )
    layer, grad, qg, kg, vg, og, gg, ug, dg, ig, pa, pf, po, qn, kn = finish(layer, grad, recv, own)
    ig, pa, pf, po, qn, kn = (item.reshape(-1) for item in (ig, pa, pf, po, qn, kn))
    return (layer, grad, qg, kg, vg, og.T, gg, ug, dg.T, ig, qn, kn, pa, pf, po)


def solution(mesh):
    in_specs = (
        P("dp", None),
        P("dp", None),
        P("dp", None),
        P("dp", None),
        P("dp", None),
        P("dp", None),
        P(None, "dp"),
        P("dp", None),
        P("dp", None),
        P(None, "dp"),
        P("dp"),
        P("dp"),
        P("dp"),
        P("dp"),
        P("dp"),
        P("dp"),
    )
    out_specs = (
        P("dp", None),
        P("dp", None),
        P("dp", None),
        P("dp", None),
        P("dp", None),
        P(None, "dp"),
        P("dp", None),
        P("dp", None),
        P(None, "dp"),
        P("dp"),
        P("dp"),
        P("dp"),
        P("dp"),
        P("dp"),
        P("dp"),
    )
    return jax.shard_map(
        per_device, mesh=mesh, in_specs=in_specs, out_specs=out_specs, check_vma=False
    )
```

```python
import functools
import math

import jax
import jax.numpy as jnp
from jax import lax
from jax.experimental import pallas as pl
from jax.experimental.pallas import tpu as pltpu
from jax.sharding import PartitionSpec as P

BF = jnp.bfloat16
F32 = jnp.float32
MESH = pl.DeviceIdType.MESH


class Place:
    def __init__(self):
        me = lax.axis_index("dp")
        self.me = me
        self.c = lax.rem(me, 2)
        self.z = lax.rem(lax.div(me, 2), 4)
        self.y = lax.rem(lax.div(me, 8), 4)
        self.x = lax.div(me, 32)
        self.yl = lax.rem(self.y, 2)
        self.yh = lax.div(self.y, 2)
        self.at = {"x": self.x, "y": self.y, "z": self.z}

    def device(self, x, y, z, c):
        return ((x * 4 + y) * 4 + z) * 2 + c

    def moved(self, axis, by):
        return lax.rem(self.at[axis] + by, 4)

    def peer(self, axis, by):
        spot = dict(self.at)
        spot[axis] = self.moved(axis, by)
        return self.device(spot["x"], spot["y"], spot["z"], self.c)

    def sibling(self):
        return self.device(self.x, self.y, self.z, 1 - self.c)

    def group_peers(self):
        found = []
        for dyl in range(2):
            for dz in range(4):
                for dc in range(2):
                    if dyl or dz or dc:
                        yl = lax.rem(self.yl + dyl, 2)
                        z = lax.rem(self.z + dz, 4)
                        c = lax.rem(self.c + dc, 2)
                        found.append(
                            (
                                self.device(self.x, self.yh * 2 + yl, z, c),
                                c * 8 + yl * 4 + z,
                                yl * 8 + z * 2 + c,
                            )
                        )
        return found

    def slot(self):
        return self.c * 8 + self.yl * 4 + self.z

    def natural(self):
        return self.yl * 8 + self.z * 2 + self.c

    def greet(self):
        others = [item[0] for item in self.group_peers()]
        others += [self.peer("x", by) for by in (1, 2, 3)]
        others += [
            self.device(self.x, (1 - self.yh) * 2 + yl, self.z, self.c) for yl in range(2)
        ]
        barrier = pltpu.get_barrier_semaphore()
        for other in others:
            pl.semaphore_signal(barrier, inc=1, device_id=(other,), device_id_type=MESH)
        self.greeted = len(others)

    def await_greetings(self):
        pl.semaphore_wait(pltpu.get_barrier_semaphore(), self.greeted)


def region(select, half=None):
    index = []
    for axis in "xyz":
        value = select[axis]
        if value is None:
            cut = half is not None
            if axis == "y":
                index += [pl.ds(half, 1) if cut else slice(None), slice(None)]
            else:
                index.append(pl.ds(2 * half, 2) if cut else slice(None))
            half = None
        elif axis == "y":
            index += [lax.div(value, 2), lax.rem(value, 2)]
        else:
            index.append(value)
    return tuple(index)


def half_shape(whole):
    shape, cut = [], True
    for axis in "xyz":
        if axis in whole:
            if axis == "y":
                shape += [1 if cut else 2, 2]
            else:
                shape.append(2 if cut else 4)
            cut = False
    return tuple(shape)


def whole_shape(whole):
    shape = []
    for axis in "xyz":
        if axis in whole:
            shape += [2, 2] if axis == "y" else [4]
    return tuple(shape)


class Sender:
    def __init__(self, send_sems, recv_sems):
        self.send_sems, self.recv_sems = send_sems, recv_sems
        self.used = 0
        self.open = []

    def send(self, source, target, device):
        copy = pltpu.make_async_remote_copy(
            src_ref=source,
            dst_ref=target,
            send_sem=self.send_sems.at[self.used],
            recv_sem=self.recv_sems.at[self.used],
            device_id=(device,),
            device_id_type=MESH,
        )
        self.used += 1
        copy.start()
        self.open.append(copy)
        return copy

    def finish(self):
        for copy in self.open:
            copy.wait_send()
        self.open = []


def gather_class(place, sender, ref, rows, order, direct):
    tail = (pl.ds(rows[0], rows[1]), slice(None))

    def view(select, half=None):
        return ref.at[(place.c,) + region(select, half) + tail]

    def select_for(step, value):
        chosen = {}
        for at, axis in enumerate(order):
            chosen[axis] = None if at < step else value if at == step else place.at[axis]
        return chosen

    def push(part, device):
        return sender.send(part, part, device)

    for step in (0, 1):
        axis = order[step]
        own = view(select_for(step, place.at[axis]))
        sent = [push(own, place.peer(axis, by)) for by in (1, 3, 2)]
        yield
        for copy in sent:
            copy.wait_recv()
    axis = order[2]
    right, left = place.peer(axis, 1), place.peer(axis, 3)
    mine = select_for(2, place.at[axis])
    of_right = select_for(2, place.moved(axis, 1))
    of_left = select_for(2, place.moved(axis, 3))
    of_far = select_for(2, place.moved(axis, 2))
    if direct:
        sent = [push(view(mine), place.peer(axis, by)) for by in (1, 3, 2)]
        twin = [push(view(mine), place.sibling())]
        yield
        for copy, part in zip(sent, (of_left, of_right, of_far)):
            copy.wait_recv()
            twin.append(push(view(part), place.sibling()))
        yield
        for copy in twin:
            copy.wait_recv()
        return
    r0 = push(view(mine, 0), right)
    l1 = push(view(mine, 1), left)
    r1 = push(view(mine, 1), right)
    l0 = push(view(mine, 0), left)
    twin = [push(view(mine), place.sibling())]
    yield
    r0.wait_recv()
    f0 = push(view(of_left, 0), right)
    l1.wait_recv()
    f1 = push(view(of_right, 1), left)
    yield
    r1.wait_recv()
    twin.append(push(view(of_left), place.sibling()))
    l0.wait_recv()
    twin.append(push(view(of_right), place.sibling()))
    yield
    f0.wait_recv()
    twin.append(push(view(of_far, 0), place.sibling()))
    f1.wait_recv()
    twin.append(push(view(of_far, 1), place.sibling()))
    yield
    for copy in twin:
        copy.wait_recv()


GATHER_COPIES = 17
SCATTER_COPIES = 16


def scatter_class(place, sender, ref, twin_ref, landing, rows, order, direct):
    tail = (pl.ds(rows[0], rows[1]), slice(None))
    order = order[::-1]

    def at(select, half=None):
        return (place.c,) + region(select, half) + tail

    def select_for(step, value):
        chosen = {}
        for where, axis in enumerate(order):
            chosen[axis] = (
                place.at[axis] if where < step else value if where == step else None
            )
        return chosen

    def add(index, *others):
        if len(others) == 1:
            ref[index] = ref[index] + others[0]
            return
        total = ref[index].astype(F32)
        for other in others:
            total = total + other.astype(F32)
        ref[index] = total.astype(BF)

    axis = order[0]
    pieces = []
    for by in (2, 1, 3, 0):
        part = region(select_for(0, place.moved(axis, by))) + tail
        pieces.append(
            (part, sender.send(ref.at[(1 - place.c,) + part], twin_ref.at[part], place.sibling()))
        )
    yield

    def joined(which):
        part, copy = pieces[which]
        copy.wait_recv()
        add((place.c,) + part, twin_ref[part])

    land = landing[0]
    right, left = place.peer(axis, 1), place.peer(axis, 3)
    mine = select_for(0, place.at[axis])
    to_right = select_for(0, place.moved(axis, 1))
    to_left = select_for(0, place.moved(axis, 3))
    far = select_for(0, place.moved(axis, 2))
    if direct:
        sent = []
        for which, by in enumerate((2, 1, 3)):
            joined(which)
            part = ref.at[at(select_for(0, place.moved(axis, by)))]
            sent.append(sender.send(part, land.at[by - 1], place.peer(axis, by)))
        joined(3)
        yield
        for copy in sent:
            copy.wait_recv()
        add(at(mine), land[0], land[1], land[2])
    else:
        joined(0)
        f0 = sender.send(ref.at[at(far, 0)], land.at[0], right)
        f1 = sender.send(ref.at[at(far, 1)], land.at[1], left)
        joined(1)
        r1 = sender.send(ref.at[at(to_right, 1)], land.at[2], right)
        joined(2)
        l0 = sender.send(ref.at[at(to_left, 0)], land.at[3], left)
        joined(3)
        yield
        f0.wait_recv()
        add(at(to_right, 0), land[0])
        r0 = sender.send(ref.at[at(to_right, 0)], land.at[4], right)
        f1.wait_recv()
        add(at(to_left, 1), land[1])
        l1 = sender.send(ref.at[at(to_left, 1)], land.at[5], left)
        yield
        r1.wait_recv()
        l0.wait_recv()
        r0.wait_recv()
        l1.wait_recv()
        add(at(mine, 0), land[4], land[3])
        add(at(mine, 1), land[2], land[5])
    for step in (1, 2):
        axis = order[step]
        land = landing[step]
        sent = [
            sender.send(
                ref.at[at(select_for(step, place.moved(axis, by)))],
                land.at[by - 1],
                place.peer(axis, by),
            )
            for by in (1, 3, 2)
        ]
        yield
        for copy in sent:
            copy.wait_recv()
        add(at(select_for(step, place.at[axis])), land[0], land[1], land[2])


def landing_shapes(rows, order, direct):
    back = order[::-1]
    return [
        pltpu.VMEM(
            ((3,) + whole_shape(back[1:]) if direct else (6,) + half_shape(back[1:])) + (rows, 128), BF
        ),
        pltpu.VMEM((3,) + whole_shape(back[2:]) + (rows, 128), BF),
        pltpu.VMEM((3, rows, 128), BF),
    ]


GAIN_ROWS = (5, 13, 21, 29, 6, 14)
PICKS = 4 * 80 + 6 * 16


def picks(row, seat):
    n = lax.shift_right_logical(seat, 5)
    inner = lax.bitwise_and(seat, 31)
    r = lax.bitwise_and(seat, 7)
    wanted = jnp.where(r < 5, lax.shift_right_logical(inner, 3) * 80 + n * 5 + r, -1)
    for at, target in enumerate(GAIN_ROWS):
        wanted = jnp.where(inner == target, 320 + at * 16 + n, wanted)
    return jnp.where(wanted == row, 1.0, 0.0).astype(BF)


def fill_pick(pick):
    for first in range(0, PICKS, 32):
        shape = (32, 512)
        pick[first : first + 32] = picks(
            lax.broadcasted_iota(jnp.int32, shape, 0) + first, lax.broadcasted_iota(jnp.int32, shape, 1)
        )


def fill_pick_t(pick_t):
    for first in range(0, 512, 32):
        shape = (32, PICKS)
        pick_t[first : first + 32] = picks(
            lax.broadcasted_iota(jnp.int32, shape, 1), lax.broadcasted_iota(jnp.int32, shape, 0) + first
        )


def stacked(parts):
    pad = jnp.zeros((3, 128), F32)
    return jnp.concatenate(
        [item for part in parts for item in (part.astype(F32), pad)], axis=0
    )


CLASSES = (
    (0, 0, 32, "xyz", False, False),
    (0, 32, 48, "yzx", False, False),
    (4, 0, 32, "zxy", False, False),
    (1, 0, 80, "xyz", False, False),
    (2, 0, 80, "yzx", False, False),
    (3, 0, 80, "zxy", False, False),
)
BLOCK_ROWS = (80, 80, 80, 80, 32)


def fill_messages(q, o, k, v, g, u, d, gains, msgs, kv_block):
    for slot in range(16):
        lanes = slice(slot * 128, slot * 128 + 128)
        narrow = slice(slot % 8 * 128, slot % 8 * 128 + 128)
        qo = q[:, narrow] if slot < 8 else o[:, narrow]
        msgs[slot] = stacked([g[:, lanes], u[:, lanes], d[:, lanes], qo]).astype(BF)
    flat = stacked([k[:, 0:128], k[:, 128:256], v[:, 0:128], v[:, 128:256]])
    row = lax.broadcasted_iota(jnp.int32, (32, 128), 0)
    for gain, target in zip(gains, GAIN_ROWS):
        flat = jnp.where(row == target, gain, flat)
    kv_block[...] = flat.astype(BF)


def exchange_start(place, sender, msgs, recv):
    return [
        sender.send(msgs.at[slot], recv.at[place.natural()], device)
        for device, slot, _ in place.group_peers()
    ]


def exchange_take(place, copies, msgs, recv, bufs, kv_block, pick):
    recv[place.natural()] = msgs[place.slot()]
    spot = (place.c, place.x, place.yh, place.yl, place.z)
    bufs[4][spot] = kv_block[...]
    for copy in copies:
        copy.wait_recv()
    flat = matmul(pick[0:320], recv[...].reshape(512, 128)).astype(BF)
    for part, buf in ((3, bufs[0]), (0, bufs[1]), (1, bufs[2]), (2, bufs[3])):
        buf[spot] = flat[part * 80 : part * 80 + 80]


def read_kv(buf, pick, kv_weight, gain_parts):
    def group(g, carry):
        x, yh = lax.div(g, 2), lax.rem(g, 2)
        blocks = [buf[c, x, yh, yl, z] for yl in range(2) for z in range(4) for c in range(2)]
        parts = matmul(pick[...], jnp.concatenate(blocks, axis=0))
        rows = pl.ds(pl.multiple_of(g * 80, 16), 80)
        for part in range(4):
            kv_weight[rows, part * 128 : part * 128 + 128] = parts[
                part * 80 : part * 80 + 80
            ].astype(BF)
        for at in range(6):
            gain_parts[at, pl.ds(pl.multiple_of(g * 16, 16), 16)] = parts[
                320 + at * 16 : 336 + at * 16
            ]
        return carry

    lax.fori_loop(0, 8, group, 0)


def owned(each, width):
    n = lax.broadcasted_iota(jnp.int32, (128, width), 0)
    inside = lax.broadcasted_iota(jnp.int32, (128, width), 1) - n * each
    return (inside >= 0) & (inside < each)


def seats(shape, lane_axis, each):
    lane = lax.broadcasted_iota(jnp.int32, shape, lane_axis)
    r = lax.broadcasted_iota(jnp.int32, shape, 1 - lane_axis)
    return jnp.where(lax.rem(lane, each) == r, 1.0, 0.0).astype(BF)


def read_gains(gain_parts, lines):
    for first, count, each, width in ((0, 4, 5, 640), (4, 2, 2, 256)):
        held = gain_parts[first : first + count].reshape(count * 128, 128).astype(BF)
        spread = matmul(held, seats((128, width), 1, each))
        mine = owned(each, width)
        for at in range(count):
            line = jnp.where(mine, spread[at * 128 : at * 128 + 128], 0.0)
            lines[first + at : first + at + 1, 0:width] = jnp.sum(line, axis=0, keepdims=True)


def fill_kv_gradient(kv, gain_lines, gain_parts, pick_t, buf):
    for at, line in enumerate(gain_lines):
        each, width = (5, 640) if at < 4 else (2, 256)
        kept = jnp.where(owned(each, width), jnp.broadcast_to(line, (128, width)), 0.0)
        gain_parts[at] = matmul(kept.astype(BF), seats((width, 128), 0, each))

    def group(g, carry):
        rows = pl.ds(pl.multiple_of(g * 80, 16), 80)
        parts = [kv[rows, part * 128 : part * 128 + 128] for part in range(4)]
        parts += [gain_parts[at, pl.ds(pl.multiple_of(g * 16, 16), 16)].astype(BF) for at in range(6)]
        flat = matmul(pick_t[...], jnp.concatenate(parts, axis=0)).astype(BF)
        x, yh = lax.div(g, 2), lax.rem(g, 2)
        for n in range(16):
            yl, z, c = n // 8, n // 2 % 4, n % 2
            buf[c, x, yh, yl, z] = flat[n * 32 : n * 32 + 32]
        return carry

    lax.fori_loop(0, 8, group, 0)


def exchange_out(place, sender, msgs, recv, bufs, pick_t):
    spot = (place.c, place.x, place.yh, place.yl, place.z)
    parts = [bufs[1][spot], bufs[2][spot], bufs[3][spot], bufs[0][spot]]
    parts.append(jnp.zeros((PICKS - 320, 128), BF))
    flat = matmul(pick_t[...], jnp.concatenate(parts, axis=0))
    msgs[...] = flat.astype(BF).reshape(16, 32, 128)
    copies = [
        sender.send(msgs.at[natural], recv.at[place.slot()], device)
        for device, _, natural in place.group_peers()
    ]
    recv[place.slot()] = msgs[place.natural()]
    for copy in copies:
        copy.wait_recv()


NORM_EPS = 1e-06
ROPE_BASE = 1000000.0
MASKED = -1e30
ROWS = 96
PACKS = 2
HEADS = 4


def matmul(left, right):
    return jnp.dot(left, right, preferred_element_type=F32)


def matmul_t(left, right):
    return lax.dot_general(left, right, (((1,), (1,)), ((), ())), preferred_element_type=F32)


def t_matmul(left, right):
    return lax.dot_general(left, right, (((0,), (0,)), ((), ())), preferred_element_type=F32)


def inverse_rms(v):
    return lax.rsqrt(jnp.mean(v * v, axis=-1, keepdims=True) + NORM_EPS)


def rms_back(v, gain, dy):
    r = inverse_rms(v)
    n = v * r
    dg = dy * gain
    dv = r * (dg - n * jnp.mean(dg * n, axis=-1, keepdims=True))
    return dv, jnp.sum(dy * n, axis=0, keepdims=True)


def turn(v, cosine, sine):
    first, second = v[:, 0:128], v[:, 128:256]
    return jnp.concatenate(
        [first * cosine - second * sine, second * cosine + first * sine], axis=1
    )


def spot_of(t):
    return lax.div(t, 4), lax.rem(lax.div(t, 2), 2), lax.rem(t, 2) * 2


def read_tile(buf, t):
    c, yl, z = spot_of(t)
    return jnp.concatenate(
        [buf[c, :, :, yl, z + k].reshape(640, 128) for k in range(2)], axis=1
    )


def write_tile(buf, t, value):
    c, yl, z = spot_of(t)
    value = value.astype(BF)
    for k in range(2):
        buf[c, :, :, yl, z + k] = value[:, k * 128 : k * 128 + 128].reshape(4, 2, 80, 128)


def tick(tasks):
    for task in list(tasks):
        try:
            next(task)
        except StopIteration:
            tasks.remove(task)


def drain(tasks):
    while tasks:
        tick(tasks)


def layer_kernel(
    tokens, segments, cotangent, q, k, v, o, g, u, d,
    input_gain, post_attn_gain, pre_ffn_gain, post_ffn_gain, query_gain, key_gain,
    layer_out, grad_tokens, part_out, kv_out,
    *scratch,
):
    weights, grads, twins = scratch[0:5], scratch[5:10], scratch[10:15]
    scratch = scratch[15:]
    landings, scratch = scratch[: 3 * len(CLASSES)], scratch[3 * len(CLASSES) :]
    (
        msgs, recv, msgs_back, recv_back, kv_block, kv_weight, kv_weight_grad, lines,
        h1_s, qraw_s, kraw_s, qf_s, kf_s, vb_s, prob_s, ctx_s, attn_s, x1_s, h2_s,
        slope_s, gelu_s, hidden_s, mixed_s, dm_s, dh2_s, dx1_s, da_s, dctx_s, dq_s, dkv_s,
        cos_s, sin_s, h2t_s, dmt_s, gain_parts, pick, pick_t,
        send_sems, recv_sems,
    ) = scratch
    place = Place()
    place.greet()
    gains = (input_gain, post_attn_gain, pre_ffn_gain, post_ffn_gain, query_gain, key_gain)
    gains = [jnp.pad(item[...].astype(F32)[None, :], ((0, 0), (0, 128 - item.shape[0]))) for item in gains]
    fill_messages(q, o, k, v, g, u, d, gains, msgs, kv_block)
    fill_pick(pick)
    sender = Sender(send_sems, recv_sems)
    place.await_greetings()
    arrivals = exchange_start(place, sender, msgs, recv)

    t_of = lax.broadcasted_iota(jnp.int32, (ROWS, ROWS), 0)
    u_of = lax.broadcasted_iota(jnp.int32, (ROWS, ROWS), 1)
    lane = lax.broadcasted_iota(jnp.int32, (1, 128), 1).astype(F32)
    frequency = jnp.exp(-math.log(ROPE_BASE) * 2.0 * lane / 256.0)
    allowed = []
    for b in range(PACKS):
        row = jnp.broadcast_to(segments[b : b + 1, :].astype(F32), (ROWS, ROWS))
        same = row == row.T
        earlier = jnp.where(same & (u_of < t_of), 1.0, 0.0)
        angles = jnp.sum(earlier, axis=1, keepdims=True) * frequency
        cos_s[b * ROWS : b * ROWS + ROWS] = jnp.cos(angles)
        sin_s[b * ROWS : b * ROWS + ROWS] = jnp.sin(angles)
        allowed.append(same & (u_of <= t_of))

    exchange_take(place, arrivals, msgs, recv, weights, kv_block, pick)

    def gather(at):
        which, first, count, order, direct, _ = CLASSES[at]
        return gather_class(place, sender, weights[which], (first, count), order, direct)

    near, wide = [gather(at) for at in range(3)], [gather(at) for at in range(3, 6)]
    tick(near)
    tick(wide)
    fill_pick_t(pick_t)
    tick(near)
    tick(wide)
    tick(near)
    tick(near)
    tick(wide)
    tick(near)
    tick(near)
    tick(near)
    tick(wide)
    read_kv(weights[4], pick, kv_weight, gain_parts)
    read_gains(gain_parts, lines)
    input_gain, post_attn_gain = lines[0:1, :], lines[1:2, :]
    pre_ffn_gain, post_ffn_gain = lines[2:3, :], lines[3:4, :]
    query_gain, key_gain = lines[4:5, 0:256], lines[5:6, 0:256]

    x = tokens[...].astype(F32)
    h1_s[...] = (x * inverse_rms(x) * input_gain).astype(BF)
    cosine, sine = cos_s[...], sin_s[...]
    h1 = h1_s[...]
    for h in range(HEADS):
        raw = matmul(h1, read_tile(weights[0], h))
        qraw_s[h] = raw
        query = turn(raw * inverse_rms(raw) * query_gain, cosine, sine) * (1.0 / 16.0)
        for b in range(PACKS):
            qf_s[b, h * ROWS : h * ROWS + ROWS] = query[b * ROWS : b * ROWS + ROWS].astype(BF)
    tick(wide)
    raw = matmul(h1, kv_weight[:, 0:256])
    kraw_s[...] = raw
    kf_s[...] = turn(raw * inverse_rms(raw) * key_gain, cosine, sine).astype(BF)
    vb_s[...] = matmul(h1, kv_weight[:, 256:512]).astype(BF)
    for b in range(PACKS):
        mine = slice(b * ROWS, b * ROWS + ROWS)
        scores = matmul_t(qf_s[b], kf_s[mine])
        scores = jnp.where(jnp.concatenate([allowed[b]] * HEADS, axis=0), scores, MASKED)
        grown = jnp.exp(scores - jnp.max(scores, axis=-1, keepdims=True))
        prob = grown / jnp.sum(grown, axis=-1, keepdims=True)
        prob_s[b] = prob
        context = matmul(prob.astype(BF), vb_s[mine]).astype(BF)
        for h in range(HEADS):
            ctx_s[h, mine] = context[h * ROWS : h * ROWS + ROWS]
    tick(wide)
    attn = matmul_t(ctx_s[0], read_tile(weights[0], 4))
    for h in range(1, HEADS):
        attn = attn + matmul_t(ctx_s[h], read_tile(weights[0], 4 + h))
    attn_s[...] = attn
    x1 = x + attn * inverse_rms(attn) * post_attn_gain
    x1_s[...] = x1
    h2_s[...] = (x1 * inverse_rms(x1) * pre_ffn_gain).astype(BF)
    h2t_s[...] = h2_s[...].astype(F32).T.astype(BF)
    tick(wide)
    drain(wide)

    mixed_s[...] = jnp.zeros((PACKS * ROWS, 640), F32)

    def feed(t, carry):
        h2 = h2_s[...]
        gate = matmul(h2, read_tile(weights[1], t))
        up = matmul(h2, read_tile(weights[2], t))
        rate = math.sqrt(2.0 / math.pi)
        square = gate * gate
        bent = jnp.tanh(rate * gate * (1.0 + 0.044715 * square))
        half = 0.5 * (1.0 + bent)
        gelu = gate * half
        slope = half + 0.5 * gate * (1.0 - bent * bent) * rate * (1.0 + 3 * 0.044715 * square)
        gelu_s[t] = gelu
        slope_s[t] = up * slope
        hidden = (gelu * up).astype(BF)
        hidden_s[t] = hidden
        mixed_s[...] += matmul_t(hidden, read_tile(weights[3], t))
        return carry

    lax.fori_loop(0, 8, feed, 0, unroll=True)

    c = cotangent[...].astype(F32)
    mixed = mixed_s[...]
    layer_out[...] = (x1_s[...] + mixed * inverse_rms(mixed) * post_ffn_gain).astype(BF)
    dm, post_ffn_line = rms_back(mixed, post_ffn_gain, c)
    dm_s[...] = dm.astype(BF)
    dmt_s[...] = dm_s[...].astype(F32).T.astype(BF)
    dh2_s[...] = jnp.zeros((PACKS * ROWS, 640), F32)

    def feed_back(t):
        dh = matmul(dm_s[...], read_tile(weights[3], t))
        dgate = (dh * slope_s[t]).astype(BF)
        dup = (dh * gelu_s[t]).astype(BF)
        dh2_s[...] += matmul_t(dgate, read_tile(weights[1], t)) + matmul_t(
            dup, read_tile(weights[2], t)
        )
        write_tile(grads[3], t, matmul(dmt_s[...], hidden_s[t]))
        write_tile(grads[1], t, matmul(h2t_s[...], dgate))
        write_tile(grads[2], t, matmul(h2t_s[...], dup))

    def first_half(i, carry):
        feed_back((1 - place.c) * 4 + i)
        return carry

    def second_half(i, carry):
        feed_back(place.c * 4 + i)
        return carry

    def scatter(at):
        which, first, count, order, _, direct = CLASSES[at]
        return scatter_class(
            place, sender, grads[which], twins[which], landings[3 * at : 3 * at + 3],
            (first, count), order, direct,
        )

    lax.fori_loop(0, 4, first_half, 0, unroll=True)
    wide = [scatter(at) for at in range(3, 6)]
    tick(wide)
    lax.fori_loop(0, 4, second_half, 0, unroll=True)
    tick(wide)

    dx1_part, pre_ffn_line = rms_back(x1_s[...], pre_ffn_gain, dh2_s[...])
    dx1 = c + dx1_part
    dx1_s[...] = dx1
    da, post_attn_line = rms_back(attn_s[...], post_attn_gain, dx1)
    da_s[...] = da.astype(BF)
    dat = da_s[...].astype(F32).T.astype(BF)
    for h in range(HEADS):
        dctx = matmul(da_s[...], read_tile(weights[0], 4 + h)).astype(BF)
        for b in range(PACKS):
            dctx_s[b, h * ROWS : h * ROWS + ROWS] = dctx[b * ROWS : b * ROWS + ROWS]
        write_tile(grads[0], 4 + h, matmul(dat, ctx_s[h]))
    query_line = jnp.zeros((1, 256), F32)
    key_line = jnp.zeros((1, 256), F32)
    for b in range(PACKS):
        mine = slice(b * ROWS, b * ROWS + ROWS)
        prob, dctx = prob_s[b], dctx_s[b]
        dp = matmul_t(dctx, vb_s[mine])
        ds = (prob * (dp - jnp.sum(prob * dp, axis=-1, keepdims=True))).astype(BF)
        dkv_s[mine, 256:512] = t_matmul(prob.astype(BF), dctx).astype(BF)
        dqf = matmul(ds, kf_s[mine]) * (1.0 / 16.0)
        dkf = t_matmul(ds, qf_s[b])
        cosine, sine = cos_s[mine, :], sin_s[mine, :]
        for h in range(HEADS):
            dq, line = rms_back(
                qraw_s[h, mine], query_gain, turn(dqf[h * ROWS : h * ROWS + ROWS], cosine, -sine)
            )
            dq_s[h, mine] = dq.astype(BF)
            query_line = query_line + line
        dk, line = rms_back(kraw_s[mine, :], key_gain, turn(dkf, cosine, -sine))
        dkv_s[mine, 0:256] = dk.astype(BF)
        key_line = key_line + line
    h1t = h1_s[...].astype(F32).T.astype(BF)
    for h in range(HEADS):
        write_tile(grads[0], h, matmul(h1t, dq_s[h]))
    near = [scatter(at) for at in range(2)]
    tick(near)
    tick(wide)
    kv_weight_grad[...] = matmul(h1t, dkv_s[...]).astype(BF)
    dh1 = matmul_t(dkv_s[...], kv_weight[...])
    for h in range(HEADS):
        dh1 = dh1 + matmul_t(dq_s[h], read_tile(weights[0], h))
    tick(near)
    x = tokens[...].astype(F32)
    dx, input_line = rms_back(x, input_gain, dh1)
    fill_kv_gradient(
        kv_weight_grad,
        (input_line, post_attn_line, pre_ffn_line, post_ffn_line, query_line, key_line),
        gain_parts, pick_t, grads[4],
    )
    last = [scatter(2)]
    tick(last)
    tick(wide)
    tick(last)
    near = near + last
    grad_tokens[...] = dx1_s[...] + dx
    while near or wide:
        tick(near)
        tick(wide)
    exchange_out(place, sender, msgs_back, recv_back, grads, pick_t)
    part_out[...] = recv_back[...]
    kv_out[...] = grads[4][place.c, place.x, place.yh, place.yl, place.z]
    sender.finish()


def run_layer(tokens, segments, cotangent, q, k, v, o_t, g, u, d_t, *gains):
    vm = pl.BlockSpec(memory_space=pltpu.VMEM)
    copies = 30 + (GATHER_COPIES + SCATTER_COPIES) * len(CLASSES)
    rows = PACKS * ROWS
    scratch = [pltpu.VMEM((2, 4, 2, 2, 4, count, 128), BF) for count in BLOCK_ROWS * 2]
    scratch += [pltpu.VMEM((4, 2, 2, 4, count, 128), BF) for count in BLOCK_ROWS]
    for _, _, count, order, _, direct in CLASSES:
        scratch += landing_shapes(count, order, direct)
    scratch += [pltpu.VMEM((16, 32, 128), BF)] * 4
    scratch += [
        pltpu.VMEM((32, 128), BF),
        pltpu.VMEM((640, 512), BF),
        pltpu.VMEM((640, 512), BF),
        pltpu.VMEM((8, 640), F32),
        pltpu.VMEM((rows, 640), BF),
        pltpu.VMEM((HEADS, rows, 256), F32),
        pltpu.VMEM((rows, 256), F32),
        pltpu.VMEM((PACKS, HEADS * ROWS, 256), BF),
        pltpu.VMEM((rows, 256), BF),
        pltpu.VMEM((rows, 256), BF),
        pltpu.VMEM((PACKS, HEADS * ROWS, ROWS), F32),
        pltpu.VMEM((HEADS, rows, 256), BF),
        pltpu.VMEM((rows, 640), F32),
        pltpu.VMEM((rows, 640), F32),
        pltpu.VMEM((rows, 640), BF),
        pltpu.VMEM((8, rows, 256), F32),
        pltpu.VMEM((8, rows, 256), F32),
        pltpu.VMEM((8, rows, 256), BF),
        pltpu.VMEM((rows, 640), F32),
        pltpu.VMEM((rows, 640), BF),
        pltpu.VMEM((rows, 640), F32),
        pltpu.VMEM((rows, 640), F32),
        pltpu.VMEM((rows, 640), BF),
        pltpu.VMEM((PACKS, HEADS * ROWS, 256), BF),
        pltpu.VMEM((HEADS, rows, 256), BF),
        pltpu.VMEM((rows, 512), BF),
        pltpu.VMEM((rows, 128), F32),
        pltpu.VMEM((rows, 128), F32),
        pltpu.VMEM((640, rows), BF),
        pltpu.VMEM((640, rows), BF),
        pltpu.VMEM((6, 128, 128), F32),
        pltpu.VMEM((PICKS, 512), BF),
        pltpu.VMEM((512, PICKS), BF),
        pltpu.SemaphoreType.DMA((copies,)),
        pltpu.SemaphoreType.DMA((copies,)),
    ]
    return pl.pallas_call(
        layer_kernel,
        out_shape=(
            jax.ShapeDtypeStruct((rows, 640), BF),
            jax.ShapeDtypeStruct((rows, 640), F32),
            jax.ShapeDtypeStruct((16, 32, 128), BF),
            jax.ShapeDtypeStruct((32, 128), BF),
        ),
        in_specs=[vm] * 16,
        out_specs=(vm,) * 4,
        scratch_shapes=scratch,
        compiler_params=pltpu.CompilerParams(
            collective_id=0, has_side_effects=True, vmem_limit_bytes=60 << 20
        ),
    )(tokens, segments, cotangent, q, k, v, o_t, g, u, d_t, *gains)


def finish_kernel(
    layer, grad, recv, own, layer_out, grad_out,
    q_out, k_out, v_out, o_out, g_out, u_out, d_out, *gain_outs,
):
    layer_out[...] = layer[...]
    grad_out[...] = grad[...]
    for slot in range(16):
        part = recv[slot].astype(F32)
        lanes = slice(slot * 128, slot * 128 + 128)
        narrow = slice(slot % 8 * 128, slot % 8 * 128 + 128)
        g_out[:, lanes] = part[0:5]
        u_out[:, lanes] = part[8:13]
        d_out[:, lanes] = part[16:21]
        (q_out if slot < 8 else o_out)[:, narrow] = part[24:29]
    flat = own[...].astype(F32)
    k_out[:, 0:128] = flat[0:5]
    k_out[:, 128:256] = flat[8:13]
    v_out[:, 0:128] = flat[16:21]
    v_out[:, 128:256] = flat[24:29]
    for out, row in zip(gain_outs, GAIN_ROWS):
        out[...] = flat[row : row + 1, 0 : out.shape[1]]


def finish(layer, grad, recv, own):
    vm = pl.BlockSpec(memory_space=pltpu.VMEM)
    shape = lambda *dims: jax.ShapeDtypeStruct(dims, F32)
    return pl.pallas_call(
        finish_kernel,
        out_shape=(
            jax.ShapeDtypeStruct(layer.shape, BF), shape(*grad.shape),
            shape(5, 1024), shape(5, 256), shape(5, 256), shape(5, 1024),
            shape(5, 2048), shape(5, 2048), shape(5, 2048),
            shape(1, 5), shape(1, 5), shape(1, 5), shape(1, 5), shape(1, 2), shape(1, 2),
        ),
        in_specs=[vm] * 4,
        out_specs=(vm,) * 15,
    )(layer, grad, recv, own)


def per_device(
    tokens,
    segment_ids,
    cotangent,
    query_weight,
    key_weight,
    value_weight,
    out_weight,
    gate_weight,
    up_weight,
    down_weight,
    input_gain,
    query_gain,
    key_gain,
    post_attn_gain,
    pre_ffn_gain,
    post_ffn_gain,
):
    layer, grad, recv, own = run_layer(
        tokens, segment_ids, cotangent, query_weight, key_weight, value_weight, out_weight.T,
        gate_weight, up_weight, down_weight.T,
        input_gain, post_attn_gain, pre_ffn_gain, post_ffn_gain, query_gain, key_gain,
    )
    layer, grad, qg, kg, vg, og, gg, ug, dg, ig, pa, pf, po, qn, kn = finish(layer, grad, recv, own)
    ig, pa, pf, po, qn, kn = (item.reshape(-1) for item in (ig, pa, pf, po, qn, kn))
    return (layer, grad, qg, kg, vg, og.T, gg, ug, dg.T, ig, qn, kn, pa, pf, po)


def solution(mesh):
    in_specs = (
        P("dp", None),
        P("dp", None),
        P("dp", None),
        P("dp", None),
        P("dp", None),
        P("dp", None),
        P(None, "dp"),
        P("dp", None),
        P("dp", None),
        P(None, "dp"),
        P("dp"),
        P("dp"),
        P("dp"),
        P("dp"),
        P("dp"),
        P("dp"),
    )
    out_specs = (
        P("dp", None),
        P("dp", None),
        P("dp", None),
        P("dp", None),
        P("dp", None),
        P(None, "dp"),
        P("dp", None),
        P("dp", None),
        P(None, "dp"),
        P("dp"),
        P("dp"),
        P("dp"),
        P("dp"),
        P("dp"),
        P("dp"),
    )
    return jax.shard_map(
        per_device, mesh=mesh, in_specs=in_specs, out_specs=out_specs, check_vma=False
    )
```

```python
import functools
import math

import jax
import jax.numpy as jnp
from jax import lax
from jax.experimental import pallas as pl
from jax.experimental.pallas import tpu as pltpu
from jax.sharding import PartitionSpec as P

BF = jnp.bfloat16
F32 = jnp.float32
MESH = pl.DeviceIdType.MESH


class Place:
    def __init__(self):
        me = lax.axis_index("dp")
        self.me = me
        self.c = lax.rem(me, 2)
        self.z = lax.rem(lax.div(me, 2), 4)
        self.y = lax.rem(lax.div(me, 8), 4)
        self.x = lax.div(me, 32)
        self.yl = lax.rem(self.y, 2)
        self.yh = lax.div(self.y, 2)
        self.at = {"x": self.x, "y": self.y, "z": self.z}

    def device(self, x, y, z, c):
        return ((x * 4 + y) * 4 + z) * 2 + c

    def moved(self, axis, by):
        return lax.rem(self.at[axis] + by, 4)

    def peer(self, axis, by):
        spot = dict(self.at)
        spot[axis] = self.moved(axis, by)
        return self.device(spot["x"], spot["y"], spot["z"], self.c)

    def sibling(self):
        return self.device(self.x, self.y, self.z, 1 - self.c)

    def group_peers(self):
        found = []
        for dyl in range(2):
            for dz in range(4):
                for dc in range(2):
                    if dyl or dz or dc:
                        yl = lax.rem(self.yl + dyl, 2)
                        z = lax.rem(self.z + dz, 4)
                        c = lax.rem(self.c + dc, 2)
                        found.append(
                            (
                                self.device(self.x, self.yh * 2 + yl, z, c),
                                c * 8 + yl * 4 + z,
                                yl * 8 + z * 2 + c,
                            )
                        )
        return found

    def slot(self):
        return self.c * 8 + self.yl * 4 + self.z

    def natural(self):
        return self.yl * 8 + self.z * 2 + self.c

    def greet(self):
        others = [item[0] for item in self.group_peers()]
        others += [self.peer("x", by) for by in (1, 2, 3)]
        others += [
            self.device(self.x, (1 - self.yh) * 2 + yl, self.z, self.c) for yl in range(2)
        ]
        barrier = pltpu.get_barrier_semaphore()
        for other in others:
            pl.semaphore_signal(barrier, inc=1, device_id=(other,), device_id_type=MESH)
        self.greeted = len(others)

    def await_greetings(self):
        pl.semaphore_wait(pltpu.get_barrier_semaphore(), self.greeted)


def region(select, half=None):
    index = []
    for axis in "xyz":
        value = select[axis]
        if value is None:
            cut = half is not None
            if axis == "y":
                index += [pl.ds(half, 1) if cut else slice(None), slice(None)]
            else:
                index.append(pl.ds(2 * half, 2) if cut else slice(None))
            half = None
        elif axis == "y":
            index += [lax.div(value, 2), lax.rem(value, 2)]
        else:
            index.append(value)
    return tuple(index)


def half_shape(whole):
    shape, cut = [], True
    for axis in "xyz":
        if axis in whole:
            if axis == "y":
                shape += [1 if cut else 2, 2]
            else:
                shape.append(2 if cut else 4)
            cut = False
    return tuple(shape)


def whole_shape(whole):
    shape = []
    for axis in "xyz":
        if axis in whole:
            shape += [2, 2] if axis == "y" else [4]
    return tuple(shape)


class Sender:
    def __init__(self, send_sems, recv_sems):
        self.send_sems, self.recv_sems = send_sems, recv_sems
        self.used = 0
        self.open = []

    def send(self, source, target, device):
        copy = pltpu.make_async_remote_copy(
            src_ref=source,
            dst_ref=target,
            send_sem=self.send_sems.at[self.used],
            recv_sem=self.recv_sems.at[self.used],
            device_id=(device,),
            device_id_type=MESH,
        )
        self.used += 1
        copy.start()
        self.open.append(copy)
        return copy

    def finish(self):
        for copy in self.open:
            copy.wait_send()
        self.open = []


def gather_class(place, sender, ref, rows, order, direct):
    tail = (pl.ds(rows[0], rows[1]), slice(None))

    def view(select, half=None):
        return ref.at[(place.c,) + region(select, half) + tail]

    def select_for(step, value):
        chosen = {}
        for at, axis in enumerate(order):
            chosen[axis] = None if at < step else value if at == step else place.at[axis]
        return chosen

    def push(part, device):
        return sender.send(part, part, device)

    for step in (0, 1):
        axis = order[step]
        own = view(select_for(step, place.at[axis]))
        sent = [push(own, place.peer(axis, by)) for by in (1, 3, 2)]
        yield
        for copy in sent:
            copy.wait_recv()
    axis = order[2]
    right, left = place.peer(axis, 1), place.peer(axis, 3)
    mine = select_for(2, place.at[axis])
    of_right = select_for(2, place.moved(axis, 1))
    of_left = select_for(2, place.moved(axis, 3))
    of_far = select_for(2, place.moved(axis, 2))
    if direct:
        sent = [push(view(mine), place.peer(axis, by)) for by in (1, 3, 2)]
        twin = [push(view(mine), place.sibling())]
        yield
        for copy, part in zip(sent, (of_left, of_right, of_far)):
            copy.wait_recv()
            twin.append(push(view(part), place.sibling()))
        yield
        for copy in twin:
            copy.wait_recv()
        return
    r0 = push(view(mine, 0), right)
    l1 = push(view(mine, 1), left)
    r1 = push(view(mine, 1), right)
    l0 = push(view(mine, 0), left)
    twin = [push(view(mine), place.sibling())]
    yield
    r0.wait_recv()
    f0 = push(view(of_left, 0), right)
    l1.wait_recv()
    f1 = push(view(of_right, 1), left)
    yield
    r1.wait_recv()
    twin.append(push(view(of_left), place.sibling()))
    l0.wait_recv()
    twin.append(push(view(of_right), place.sibling()))
    yield
    f0.wait_recv()
    twin.append(push(view(of_far, 0), place.sibling()))
    f1.wait_recv()
    twin.append(push(view(of_far, 1), place.sibling()))
    yield
    for copy in twin:
        copy.wait_recv()


GATHER_COPIES = 17
SCATTER_COPIES = 16


def scatter_class(place, sender, ref, twin_ref, landing, rows, order, direct):
    tail = (pl.ds(rows[0], rows[1]), slice(None))
    order = order[::-1]

    def at(select, half=None):
        return (place.c,) + region(select, half) + tail

    def select_for(step, value):
        chosen = {}
        for where, axis in enumerate(order):
            chosen[axis] = (
                place.at[axis] if where < step else value if where == step else None
            )
        return chosen

    def add(index, *others):
        if len(others) == 1:
            ref[index] = ref[index] + others[0]
            return
        total = ref[index].astype(F32)
        for other in others:
            total = total + other.astype(F32)
        ref[index] = total.astype(BF)

    axis = order[0]
    pieces = []
    for by in (2, 1, 3, 0):
        part = region(select_for(0, place.moved(axis, by))) + tail
        pieces.append(
            (part, sender.send(ref.at[(1 - place.c,) + part], twin_ref.at[part], place.sibling()))
        )
    yield

    def joined(which):
        part, copy = pieces[which]
        copy.wait_recv()
        add((place.c,) + part, twin_ref[part])

    land = landing[0]
    right, left = place.peer(axis, 1), place.peer(axis, 3)
    mine = select_for(0, place.at[axis])
    to_right = select_for(0, place.moved(axis, 1))
    to_left = select_for(0, place.moved(axis, 3))
    far = select_for(0, place.moved(axis, 2))
    if direct:
        sent = []
        for which, by in enumerate((2, 1, 3)):
            joined(which)
            part = ref.at[at(select_for(0, place.moved(axis, by)))]
            sent.append(sender.send(part, land.at[by - 1], place.peer(axis, by)))
        joined(3)
        yield
        for copy in sent:
            copy.wait_recv()
        add(at(mine), land[0], land[1], land[2])
    else:
        joined(0)
        f0 = sender.send(ref.at[at(far, 0)], land.at[0], right)
        f1 = sender.send(ref.at[at(far, 1)], land.at[1], left)
        joined(1)
        r1 = sender.send(ref.at[at(to_right, 1)], land.at[2], right)
        joined(2)
        l0 = sender.send(ref.at[at(to_left, 0)], land.at[3], left)
        joined(3)
        yield
        f0.wait_recv()
        add(at(to_right, 0), land[0])
        r0 = sender.send(ref.at[at(to_right, 0)], land.at[4], right)
        f1.wait_recv()
        add(at(to_left, 1), land[1])
        l1 = sender.send(ref.at[at(to_left, 1)], land.at[5], left)
        yield
        r1.wait_recv()
        l0.wait_recv()
        r0.wait_recv()
        l1.wait_recv()
        add(at(mine, 0), land[4], land[3])
        add(at(mine, 1), land[2], land[5])
    for step in (1, 2):
        axis = order[step]
        land = landing[step]
        sent = [
            sender.send(
                ref.at[at(select_for(step, place.moved(axis, by)))],
                land.at[by - 1],
                place.peer(axis, by),
            )
            for by in (1, 3, 2)
        ]
        yield
        for copy in sent:
            copy.wait_recv()
        add(at(select_for(step, place.at[axis])), land[0], land[1], land[2])


def landing_shapes(rows, order, direct):
    back = order[::-1]
    return [
        pltpu.VMEM(
            ((3,) + whole_shape(back[1:]) if direct else (6,) + half_shape(back[1:])) + (rows, 128), BF
        ),
        pltpu.VMEM((3,) + whole_shape(back[2:]) + (rows, 128), BF),
        pltpu.VMEM((3, rows, 128), BF),
    ]


GAIN_ROWS = (5, 13, 21, 29, 6, 14)
PICKS = 4 * 80 + 6 * 16


def picks(row, seat):
    n = lax.shift_right_logical(seat, 5)
    inner = lax.bitwise_and(seat, 31)
    r = lax.bitwise_and(seat, 7)
    wanted = jnp.where(r < 5, lax.shift_right_logical(inner, 3) * 80 + n * 5 + r, -1)
    for at, target in enumerate(GAIN_ROWS):
        wanted = jnp.where(inner == target, 320 + at * 16 + n, wanted)
    return jnp.where(wanted == row, 1.0, 0.0).astype(BF)


def fill_pick(pick):
    for first in range(0, PICKS, 32):
        shape = (32, 512)
        pick[first : first + 32] = picks(
            lax.broadcasted_iota(jnp.int32, shape, 0) + first, lax.broadcasted_iota(jnp.int32, shape, 1)
        )


def fill_pick_t(pick_t):
    for first in range(0, 512, 32):
        shape = (32, PICKS)
        pick_t[first : first + 32] = picks(
            lax.broadcasted_iota(jnp.int32, shape, 1), lax.broadcasted_iota(jnp.int32, shape, 0) + first
        )


def stacked(parts):
    pad = jnp.zeros((3, 128), F32)
    return jnp.concatenate(
        [item for part in parts for item in (part.astype(F32), pad)], axis=0
    )


CLASSES = (
    (0, 0, 32, "xyz", False, False),
    (0, 32, 48, "yzx", False, False),
    (4, 0, 32, "zxy", False, False),
    (1, 0, 80, "xyz", False, False),
    (2, 0, 80, "yzx", False, False),
    (3, 0, 80, "zxy", False, False),
)
BLOCK_ROWS = (80, 80, 80, 80, 32)


def fill_messages(q, o, k, v, g, u, d, gains, msgs, kv_block):
    for slot in range(16):
        lanes = slice(slot * 128, slot * 128 + 128)
        narrow = slice(slot % 8 * 128, slot % 8 * 128 + 128)
        qo = q[:, narrow] if slot < 8 else o[:, narrow]
        msgs[slot] = stacked([g[:, lanes], u[:, lanes], d[:, lanes], qo]).astype(BF)
    flat = stacked([k[:, 0:128], k[:, 128:256], v[:, 0:128], v[:, 128:256]])
    row = lax.broadcasted_iota(jnp.int32, (32, 128), 0)
    for gain, target in zip(gains, GAIN_ROWS):
        flat = jnp.where(row == target, gain, flat)
    kv_block[...] = flat.astype(BF)


def exchange_start(place, sender, msgs, recv):
    return [
        sender.send(msgs.at[slot], recv.at[place.natural()], device)
        for device, slot, _ in place.group_peers()
    ]


def exchange_take(place, copies, msgs, recv, bufs, kv_block, pick):
    recv[place.natural()] = msgs[place.slot()]
    spot = (place.c, place.x, place.yh, place.yl, place.z)
    bufs[4][spot] = kv_block[...]
    for copy in copies:
        copy.wait_recv()
    flat = matmul(pick[0:320], recv[...].reshape(512, 128)).astype(BF)
    for part, buf in ((3, bufs[0]), (0, bufs[1]), (1, bufs[2]), (2, bufs[3])):
        buf[spot] = flat[part * 80 : part * 80 + 80]


def read_kv(buf, pick, kv_weight, gain_parts):
    def group(g, carry):
        x, yh = lax.div(g, 2), lax.rem(g, 2)
        blocks = [buf[c, x, yh, yl, z] for yl in range(2) for z in range(4) for c in range(2)]
        parts = matmul(pick[...], jnp.concatenate(blocks, axis=0))
        rows = pl.ds(pl.multiple_of(g * 80, 16), 80)
        for part in range(4):
            kv_weight[rows, part * 128 : part * 128 + 128] = parts[
                part * 80 : part * 80 + 80
            ].astype(BF)
        for at in range(6):
            gain_parts[at, pl.ds(pl.multiple_of(g * 16, 16), 16)] = parts[
                320 + at * 16 : 336 + at * 16
            ]
        return carry

    lax.fori_loop(0, 8, group, 0)


def owned(each, width):
    n = lax.broadcasted_iota(jnp.int32, (128, width), 0)
    inside = lax.broadcasted_iota(jnp.int32, (128, width), 1) - n * each
    return (inside >= 0) & (inside < each)


def seats(shape, lane_axis, each):
    lane = lax.broadcasted_iota(jnp.int32, shape, lane_axis)
    r = lax.broadcasted_iota(jnp.int32, shape, 1 - lane_axis)
    return jnp.where(lax.rem(lane, each) == r, 1.0, 0.0).astype(BF)


def read_gains(gain_parts, lines):
    for first, count, each, width in ((0, 4, 5, 640), (4, 2, 2, 256)):
        held = gain_parts[first : first + count].reshape(count * 128, 128).astype(BF)
        spread = matmul(held, seats((128, width), 1, each))
        mine = owned(each, width)
        for at in range(count):
            line = jnp.where(mine, spread[at * 128 : at * 128 + 128], 0.0)
            lines[first + at : first + at + 1, 0:width] = jnp.sum(line, axis=0, keepdims=True)


def fill_kv_gradient(kv, gain_lines, gain_parts, pick_t, buf):
    for at, line in enumerate(gain_lines):
        each, width = (5, 640) if at < 4 else (2, 256)
        kept = jnp.where(owned(each, width), jnp.broadcast_to(line, (128, width)), 0.0)
        gain_parts[at] = matmul(kept.astype(BF), seats((width, 128), 0, each))

    def group(g, carry):
        rows = pl.ds(pl.multiple_of(g * 80, 16), 80)
        parts = [kv[rows, part * 128 : part * 128 + 128] for part in range(4)]
        parts += [gain_parts[at, pl.ds(pl.multiple_of(g * 16, 16), 16)].astype(BF) for at in range(6)]
        flat = matmul(pick_t[...], jnp.concatenate(parts, axis=0)).astype(BF)
        x, yh = lax.div(g, 2), lax.rem(g, 2)
        for n in range(16):
            yl, z, c = n // 8, n // 2 % 4, n % 2
            buf[c, x, yh, yl, z] = flat[n * 32 : n * 32 + 32]
        return carry

    lax.fori_loop(0, 8, group, 0)


def exchange_out(place, sender, msgs, recv, bufs, pick_t):
    spot = (place.c, place.x, place.yh, place.yl, place.z)
    parts = [bufs[1][spot], bufs[2][spot], bufs[3][spot], bufs[0][spot]]
    parts.append(jnp.zeros((PICKS - 320, 128), BF))
    flat = matmul(pick_t[...], jnp.concatenate(parts, axis=0))
    msgs[...] = flat.astype(BF).reshape(16, 32, 128)
    copies = [
        sender.send(msgs.at[natural], recv.at[place.slot()], device)
        for device, _, natural in place.group_peers()
    ]
    recv[place.slot()] = msgs[place.natural()]
    for copy in copies:
        copy.wait_recv()


NORM_EPS = 1e-06
ROPE_BASE = 1000000.0
MASKED = -1e30
ROWS = 96
PACKS = 2
HEADS = 4


def matmul(left, right):
    return jnp.dot(left, right, preferred_element_type=F32)


def matmul_t(left, right):
    return lax.dot_general(left, right, (((1,), (1,)), ((), ())), preferred_element_type=F32)


def t_matmul(left, right):
    return lax.dot_general(left, right, (((0,), (0,)), ((), ())), preferred_element_type=F32)


def inverse_rms(v):
    return lax.rsqrt(jnp.mean(v * v, axis=-1, keepdims=True) + NORM_EPS)


def rms_back(v, gain, dy):
    r = inverse_rms(v)
    n = v * r
    dg = dy * gain
    dv = r * (dg - n * jnp.mean(dg * n, axis=-1, keepdims=True))
    return dv, jnp.sum(dy * n, axis=0, keepdims=True)


def turn(v, cosine, sine):
    first, second = v[:, 0:128], v[:, 128:256]
    return jnp.concatenate(
        [first * cosine - second * sine, second * cosine + first * sine], axis=1
    )


def spot_of(t):
    return lax.div(t, 4), lax.rem(lax.div(t, 2), 2), lax.rem(t, 2) * 2


def read_tile(buf, t):
    c, yl, z = spot_of(t)
    return jnp.concatenate(
        [buf[c, :, :, yl, z + k].reshape(640, 128) for k in range(2)], axis=1
    )


def write_tile(buf, t, value):
    c, yl, z = spot_of(t)
    value = value.astype(BF)
    for k in range(2):
        buf[c, :, :, yl, z + k] = value[:, k * 128 : k * 128 + 128].reshape(4, 2, 80, 128)


def tick(tasks):
    for task in list(tasks):
        try:
            next(task)
        except StopIteration:
            tasks.remove(task)


def drain(tasks):
    while tasks:
        tick(tasks)


def layer_kernel(
    tokens, segments, cotangent, q, k, v, o, g, u, d,
    input_gain, post_attn_gain, pre_ffn_gain, post_ffn_gain, query_gain, key_gain,
    layer_out, grad_tokens, part_out, kv_out,
    *scratch,
):
    weights, grads, twins = scratch[0:5], scratch[5:10], scratch[10:15]
    scratch = scratch[15:]
    landings, scratch = scratch[: 3 * len(CLASSES)], scratch[3 * len(CLASSES) :]
    (
        msgs, recv, msgs_back, recv_back, kv_block, kv_weight, kv_weight_grad, lines,
        h1_s, qraw_s, kraw_s, qf_s, kf_s, vb_s, prob_s, ctx_s, attn_s, x1_s, h2_s,
        slope_s, gelu_s, hidden_s, mixed_s, dm_s, dh2_s, dx1_s, da_s, dctx_s, dq_s, dkv_s,
        cos_s, sin_s, h2t_s, dmt_s, gain_parts, pick, pick_t,
        send_sems, recv_sems,
    ) = scratch
    place = Place()
    place.greet()
    gains = (input_gain, post_attn_gain, pre_ffn_gain, post_ffn_gain, query_gain, key_gain)
    gains = [jnp.pad(item[...].astype(F32)[None, :], ((0, 0), (0, 128 - item.shape[0]))) for item in gains]
    fill_messages(q, o, k, v, g, u, d, gains, msgs, kv_block)
    fill_pick(pick)
    sender = Sender(send_sems, recv_sems)
    place.await_greetings()
    arrivals = exchange_start(place, sender, msgs, recv)

    t_of = lax.broadcasted_iota(jnp.int32, (ROWS, ROWS), 0)
    u_of = lax.broadcasted_iota(jnp.int32, (ROWS, ROWS), 1)
    lane = lax.broadcasted_iota(jnp.int32, (1, 128), 1).astype(F32)
    frequency = jnp.exp(-math.log(ROPE_BASE) * 2.0 * lane / 256.0)
    allowed = []
    for b in range(PACKS):
        row = jnp.broadcast_to(segments[b : b + 1, :].astype(F32), (ROWS, ROWS))
        same = row == row.T
        earlier = jnp.where(same & (u_of < t_of), 1.0, 0.0)
        angles = jnp.sum(earlier, axis=1, keepdims=True) * frequency
        cos_s[b * ROWS : b * ROWS + ROWS] = jnp.cos(angles)
        sin_s[b * ROWS : b * ROWS + ROWS] = jnp.sin(angles)
        allowed.append(same & (u_of <= t_of))

    exchange_take(place, arrivals, msgs, recv, weights, kv_block, pick)

    def gather(at):
        which, first, count, order, direct, _ = CLASSES[at]
        return gather_class(place, sender, weights[which], (first, count), order, direct)

    near, wide = [gather(at) for at in range(3)], [gather(at) for at in range(3, 6)]
    tick(near)
    tick(wide)
    fill_pick_t(pick_t)
    tick(near)
    tick(wide)
    tick(near)
    tick(near)
    tick(wide)
    tick(near)
    tick(near)
    tick(near)
    tick(wide)
    read_kv(weights[4], pick, kv_weight, gain_parts)
    read_gains(gain_parts, lines)
    input_gain, post_attn_gain = lines[0:1, :], lines[1:2, :]
    pre_ffn_gain, post_ffn_gain = lines[2:3, :], lines[3:4, :]
    query_gain, key_gain = lines[4:5, 0:256], lines[5:6, 0:256]

    x = tokens[...].astype(F32)
    h1_s[...] = (x * inverse_rms(x) * input_gain).astype(BF)
    cosine, sine = cos_s[...], sin_s[...]
    h1 = h1_s[...]
    for h in range(HEADS):
        raw = matmul(h1, read_tile(weights[0], h))
        qraw_s[h] = raw
        query = turn(raw * inverse_rms(raw) * query_gain, cosine, sine) * (1.0 / 16.0)
        for b in range(PACKS):
            qf_s[b, h * ROWS : h * ROWS + ROWS] = query[b * ROWS : b * ROWS + ROWS].astype(BF)
    tick(wide)
    raw = matmul(h1, kv_weight[:, 0:256])
    kraw_s[...] = raw
    kf_s[...] = turn(raw * inverse_rms(raw) * key_gain, cosine, sine).astype(BF)
    vb_s[...] = matmul(h1, kv_weight[:, 256:512]).astype(BF)
    for b in range(PACKS):
        mine = slice(b * ROWS, b * ROWS + ROWS)
        scores = matmul_t(qf_s[b], kf_s[mine])
        scores = jnp.where(jnp.concatenate([allowed[b]] * HEADS, axis=0), scores, MASKED)
        grown = jnp.exp(scores - jnp.max(scores, axis=-1, keepdims=True))
        prob = grown / jnp.sum(grown, axis=-1, keepdims=True)
        prob_s[b] = prob
        context = matmul(prob.astype(BF), vb_s[mine]).astype(BF)
        for h in range(HEADS):
            ctx_s[h, mine] = context[h * ROWS : h * ROWS + ROWS]
    tick(wide)
    attn = matmul_t(ctx_s[0], read_tile(weights[0], 4))
    for h in range(1, HEADS):
        attn = attn + matmul_t(ctx_s[h], read_tile(weights[0], 4 + h))
    attn_s[...] = attn
    x1 = x + attn * inverse_rms(attn) * post_attn_gain
    x1_s[...] = x1
    h2_s[...] = (x1 * inverse_rms(x1) * pre_ffn_gain).astype(BF)
    h2t_s[...] = h2_s[...].astype(F32).T.astype(BF)
    tick(wide)
    drain(wide)

    mixed_s[...] = jnp.zeros((PACKS * ROWS, 640), F32)

    def feed(t, carry):
        h2 = h2_s[...]
        gate = matmul(h2, read_tile(weights[1], t))
        up = matmul(h2, read_tile(weights[2], t))
        rate = math.sqrt(2.0 / math.pi)
        square = gate * gate
        bent = jnp.tanh(rate * gate * (1.0 + 0.044715 * square))
        half = 0.5 * (1.0 + bent)
        gelu = gate * half
        slope = half + 0.5 * gate * (1.0 - bent * bent) * rate * (1.0 + 3 * 0.044715 * square)
        gelu_s[t] = gelu
        slope_s[t] = up * slope
        hidden = (gelu * up).astype(BF)
        hidden_s[t] = hidden
        return carry

    lax.fori_loop(0, 8, feed, 0, unroll=True)

    c = cotangent[...].astype(F32)
    mixed = matmul_t(hidden_s[0], read_tile(weights[3], 0))
    for t in range(1, 8):
        mixed = mixed + matmul_t(hidden_s[t], read_tile(weights[3], t))
    layer_out[...] = (x1_s[...] + mixed * inverse_rms(mixed) * post_ffn_gain).astype(BF)
    dm, post_ffn_line = rms_back(mixed, post_ffn_gain, c)
    dm_s[...] = dm.astype(BF)
    dmt_s[...] = dm_s[...].astype(F32).T.astype(BF)
    dh2_s[...] = jnp.zeros((PACKS * ROWS, 640), F32)

    def feed_back(t):
        dh = matmul(dm_s[...], read_tile(weights[3], t))
        dgate = (dh * slope_s[t]).astype(BF)
        dup = (dh * gelu_s[t]).astype(BF)
        dh2_s[...] += matmul_t(dgate, read_tile(weights[1], t)) + matmul_t(
            dup, read_tile(weights[2], t)
        )
        write_tile(grads[3], t, matmul(dmt_s[...], hidden_s[t]))
        write_tile(grads[1], t, matmul(h2t_s[...], dgate))
        write_tile(grads[2], t, matmul(h2t_s[...], dup))

    def first_half(i, carry):
        feed_back((1 - place.c) * 4 + i)
        return carry

    def second_half(i, carry):
        feed_back(place.c * 4 + i)
        return carry

    def scatter(at):
        which, first, count, order, _, direct = CLASSES[at]
        return scatter_class(
            place, sender, grads[which], twins[which], landings[3 * at : 3 * at + 3],
            (first, count), order, direct,
        )

    lax.fori_loop(0, 4, first_half, 0, unroll=True)
    wide = [scatter(at) for at in range(3, 6)]
    tick(wide)
    lax.fori_loop(0, 4, second_half, 0, unroll=True)
    tick(wide)

    dx1_part, pre_ffn_line = rms_back(x1_s[...], pre_ffn_gain, dh2_s[...])
    dx1 = c + dx1_part
    dx1_s[...] = dx1
    da, post_attn_line = rms_back(attn_s[...], post_attn_gain, dx1)
    da_s[...] = da.astype(BF)
    dat = da_s[...].astype(F32).T.astype(BF)
    for h in range(HEADS):
        dctx = matmul(da_s[...], read_tile(weights[0], 4 + h)).astype(BF)
        for b in range(PACKS):
            dctx_s[b, h * ROWS : h * ROWS + ROWS] = dctx[b * ROWS : b * ROWS + ROWS]
        write_tile(grads[0], 4 + h, matmul(dat, ctx_s[h]))
    query_line = jnp.zeros((1, 256), F32)
    key_line = jnp.zeros((1, 256), F32)
    for b in range(PACKS):
        mine = slice(b * ROWS, b * ROWS + ROWS)
        prob, dctx = prob_s[b], dctx_s[b]
        dp = matmul_t(dctx, vb_s[mine])
        ds = (prob * (dp - jnp.sum(prob * dp, axis=-1, keepdims=True))).astype(BF)
        dkv_s[mine, 256:512] = t_matmul(prob.astype(BF), dctx).astype(BF)
        dqf = matmul(ds, kf_s[mine]) * (1.0 / 16.0)
        dkf = t_matmul(ds, qf_s[b])
        cosine, sine = cos_s[mine, :], sin_s[mine, :]
        for h in range(HEADS):
            dq, line = rms_back(
                qraw_s[h, mine], query_gain, turn(dqf[h * ROWS : h * ROWS + ROWS], cosine, -sine)
            )
            dq_s[h, mine] = dq.astype(BF)
            query_line = query_line + line
        dk, line = rms_back(kraw_s[mine, :], key_gain, turn(dkf, cosine, -sine))
        dkv_s[mine, 0:256] = dk.astype(BF)
        key_line = key_line + line
    h1t = h1_s[...].astype(F32).T.astype(BF)
    for h in range(HEADS):
        write_tile(grads[0], h, matmul(h1t, dq_s[h]))
    near = [scatter(at) for at in range(2)]
    tick(near)
    tick(wide)
    kv_weight_grad[...] = matmul(h1t, dkv_s[...]).astype(BF)
    dh1 = matmul_t(dkv_s[...], kv_weight[...])
    for h in range(HEADS):
        dh1 = dh1 + matmul_t(dq_s[h], read_tile(weights[0], h))
    tick(near)
    x = tokens[...].astype(F32)
    dx, input_line = rms_back(x, input_gain, dh1)
    fill_kv_gradient(
        kv_weight_grad,
        (input_line, post_attn_line, pre_ffn_line, post_ffn_line, query_line, key_line),
        gain_parts, pick_t, grads[4],
    )
    last = [scatter(2)]
    tick(last)
    tick(wide)
    tick(last)
    near = near + last
    grad_tokens[...] = dx1_s[...] + dx
    while near or wide:
        tick(near)
        tick(wide)
    exchange_out(place, sender, msgs_back, recv_back, grads, pick_t)
    part_out[...] = recv_back[...]
    kv_out[...] = grads[4][place.c, place.x, place.yh, place.yl, place.z]
    sender.finish()


def run_layer(tokens, segments, cotangent, q, k, v, o_t, g, u, d_t, *gains):
    vm = pl.BlockSpec(memory_space=pltpu.VMEM)
    copies = 30 + (GATHER_COPIES + SCATTER_COPIES) * len(CLASSES)
    rows = PACKS * ROWS
    scratch = [pltpu.VMEM((2, 4, 2, 2, 4, count, 128), BF) for count in BLOCK_ROWS * 2]
    scratch += [pltpu.VMEM((4, 2, 2, 4, count, 128), BF) for count in BLOCK_ROWS]
    for _, _, count, order, _, direct in CLASSES:
        scratch += landing_shapes(count, order, direct)
    scratch += [pltpu.VMEM((16, 32, 128), BF)] * 4
    scratch += [
        pltpu.VMEM((32, 128), BF),
        pltpu.VMEM((640, 512), BF),
        pltpu.VMEM((640, 512), BF),
        pltpu.VMEM((8, 640), F32),
        pltpu.VMEM((rows, 640), BF),
        pltpu.VMEM((HEADS, rows, 256), F32),
        pltpu.VMEM((rows, 256), F32),
        pltpu.VMEM((PACKS, HEADS * ROWS, 256), BF),
        pltpu.VMEM((rows, 256), BF),
        pltpu.VMEM((rows, 256), BF),
        pltpu.VMEM((PACKS, HEADS * ROWS, ROWS), F32),
        pltpu.VMEM((HEADS, rows, 256), BF),
        pltpu.VMEM((rows, 640), F32),
        pltpu.VMEM((rows, 640), F32),
        pltpu.VMEM((rows, 640), BF),
        pltpu.VMEM((8, rows, 256), F32),
        pltpu.VMEM((8, rows, 256), F32),
        pltpu.VMEM((8, rows, 256), BF),
        pltpu.VMEM((rows, 640), F32),
        pltpu.VMEM((rows, 640), BF),
        pltpu.VMEM((rows, 640), F32),
        pltpu.VMEM((rows, 640), F32),
        pltpu.VMEM((rows, 640), BF),
        pltpu.VMEM((PACKS, HEADS * ROWS, 256), BF),
        pltpu.VMEM((HEADS, rows, 256), BF),
        pltpu.VMEM((rows, 512), BF),
        pltpu.VMEM((rows, 128), F32),
        pltpu.VMEM((rows, 128), F32),
        pltpu.VMEM((640, rows), BF),
        pltpu.VMEM((640, rows), BF),
        pltpu.VMEM((6, 128, 128), F32),
        pltpu.VMEM((PICKS, 512), BF),
        pltpu.VMEM((512, PICKS), BF),
        pltpu.SemaphoreType.DMA((copies,)),
        pltpu.SemaphoreType.DMA((copies,)),
    ]
    return pl.pallas_call(
        layer_kernel,
        out_shape=(
            jax.ShapeDtypeStruct((rows, 640), BF),
            jax.ShapeDtypeStruct((rows, 640), F32),
            jax.ShapeDtypeStruct((16, 32, 128), BF),
            jax.ShapeDtypeStruct((32, 128), BF),
        ),
        in_specs=[vm] * 16,
        out_specs=(vm,) * 4,
        scratch_shapes=scratch,
        compiler_params=pltpu.CompilerParams(
            collective_id=0, has_side_effects=True, vmem_limit_bytes=60 << 20
        ),
    )(tokens, segments, cotangent, q, k, v, o_t, g, u, d_t, *gains)


def finish_kernel(
    layer, grad, recv, own, layer_out, grad_out,
    q_out, k_out, v_out, o_out, g_out, u_out, d_out, *gain_outs,
):
    layer_out[...] = layer[...]
    grad_out[...] = grad[...]
    for slot in range(16):
        part = recv[slot].astype(F32)
        lanes = slice(slot * 128, slot * 128 + 128)
        narrow = slice(slot % 8 * 128, slot % 8 * 128 + 128)
        g_out[:, lanes] = part[0:5]
        u_out[:, lanes] = part[8:13]
        d_out[:, lanes] = part[16:21]
        (q_out if slot < 8 else o_out)[:, narrow] = part[24:29]
    flat = own[...].astype(F32)
    k_out[:, 0:128] = flat[0:5]
    k_out[:, 128:256] = flat[8:13]
    v_out[:, 0:128] = flat[16:21]
    v_out[:, 128:256] = flat[24:29]
    for out, row in zip(gain_outs, GAIN_ROWS):
        out[...] = flat[row : row + 1, 0 : out.shape[1]]


def finish(layer, grad, recv, own):
    vm = pl.BlockSpec(memory_space=pltpu.VMEM)
    shape = lambda *dims: jax.ShapeDtypeStruct(dims, F32)
    return pl.pallas_call(
        finish_kernel,
        out_shape=(
            jax.ShapeDtypeStruct(layer.shape, BF), shape(*grad.shape),
            shape(5, 1024), shape(5, 256), shape(5, 256), shape(5, 1024),
            shape(5, 2048), shape(5, 2048), shape(5, 2048),
            shape(1, 5), shape(1, 5), shape(1, 5), shape(1, 5), shape(1, 2), shape(1, 2),
        ),
        in_specs=[vm] * 4,
        out_specs=(vm,) * 15,
    )(layer, grad, recv, own)


def per_device(
    tokens,
    segment_ids,
    cotangent,
    query_weight,
    key_weight,
    value_weight,
    out_weight,
    gate_weight,
    up_weight,
    down_weight,
    input_gain,
    query_gain,
    key_gain,
    post_attn_gain,
    pre_ffn_gain,
    post_ffn_gain,
):
    layer, grad, recv, own = run_layer(
        tokens, segment_ids, cotangent, query_weight, key_weight, value_weight, out_weight.T,
        gate_weight, up_weight, down_weight.T,
        input_gain, post_attn_gain, pre_ffn_gain, post_ffn_gain, query_gain, key_gain,
    )
    layer, grad, qg, kg, vg, og, gg, ug, dg, ig, pa, pf, po, qn, kn = finish(layer, grad, recv, own)
    ig, pa, pf, po, qn, kn = (item.reshape(-1) for item in (ig, pa, pf, po, qn, kn))
    return (layer, grad, qg, kg, vg, og.T, gg, ug, dg.T, ig, qn, kn, pa, pf, po)


def solution(mesh):
    in_specs = (
        P("dp", None),
        P("dp", None),
        P("dp", None),
        P("dp", None),
        P("dp", None),
        P("dp", None),
        P(None, "dp"),
        P("dp", None),
        P("dp", None),
        P(None, "dp"),
        P("dp"),
        P("dp"),
        P("dp"),
        P("dp"),
        P("dp"),
        P("dp"),
    )
    out_specs = (
        P("dp", None),
        P("dp", None),
        P("dp", None),
        P("dp", None),
        P("dp", None),
        P(None, "dp"),
        P("dp", None),
        P("dp", None),
        P(None, "dp"),
        P("dp"),
        P("dp"),
        P("dp"),
        P("dp"),
        P("dp"),
        P("dp"),
    )
    return jax.shard_map(
        per_device, mesh=mesh, in_specs=in_specs, out_specs=out_specs, check_vma=False
    )
```
